32 devices in a mesh: row: 4 (over y, x), col: 8 (over z, core).
Axes of the slice: x: 2, y: 2, z: 4, core: 2. Of those that a mesh axis runs over, the one named last changes fastest.
Arguments:
- positions: float32 [3, 32768], P(None, ('row', 'col')), may hold values from 0 to 1
- strengths: float32 [3, 32768], P(None, ('row', 'col')), may hold values from -0.06 to 0.06
- radii: float32 [32768], P(('row', 'col')), may hold values from 0.1 to 0.3
- pair_list: int32 [2, 4, 8, 2], P(None, 'row', 'col'), may hold values from 0 to 7, as said below
- pair_count: int32 [4, 8], P('row', 'col'), may hold values from 1 to 2, as said below
Outputs:
- velocity: float32 [3, 32768], P(None, ('row', 'col'))
- stretching: float32 [3, 32768], P(None, ('row', 'col'))
The draws below stay inside these ranges and needn't reach their ends.
Inputs may be any that keep to these rules, and one draw needn't show every extreme that they name: `pair_list`: row-block indices lie in 0 to 7, column-block indices in 0 to 3; slot 0 of every tile pairs a group with itself. `pair_count`: some tile fills all 2 slots.
All inputs are finite; a program needn't handle non-finite values.
Results may differ from the reference program's by a relative error of at most 0.0003.
Values sent between devices are 32-bit elements; how exact they have to be, the bound alone decides.
No kernel may reach another device: no remote copies, remote signals or barrier semaphores. Data moves between devices by JAX's collectives and lax.ppermute only.
A program may use at most 192 MiB of HBM per device.

```python
import math
import jax
import jax.numpy as jnp
from jax import lax

G = 1024
GD = 1
PMAX = 2
NP = 32768
N_ROW = 4
N_COL = 8


def draw_pair_list(key, part):
    key = jax.random.fold_in(key, 11)
    k_row, k_col, k_diag = jax.random.split(key, 3)
    rows_part = jax.random.randint(k_row, (N_ROW, N_COL, PMAX), 0, GD * N_COL)
    cols_part = jax.random.randint(k_col, (N_ROW, N_COL, PMAX), 0, GD * N_ROW)
    offset = jax.random.randint(k_diag, (N_ROW, N_COL), 0, GD)
    rows_i = jnp.arange(N_ROW, dtype=jnp.int32)[:, None]
    cols_i = jnp.arange(N_COL, dtype=jnp.int32)[None, :]
    rows_part = rows_part.at[:, :, 0].set(cols_i * GD + offset)
    cols_part = cols_part.at[:, :, 0].set(rows_i * GD + offset)
    return jnp.stack([rows_part, cols_part]).astype(jnp.int32)


def draw_pair_count(key, part):
    key = jax.random.fold_in(key, 23)
    k_base, k_full = jax.random.split(key, 2)
    lowest = max(1, (PMAX + 1) // 2)
    counts = jax.random.randint(k_base, (N_ROW * N_COL,), lowest, PMAX + 1)
    full = jax.random.randint(k_full, (), 0, N_ROW * N_COL)
    counts = counts.at[full].set(PMAX)
    return counts.reshape(N_ROW, N_COL).astype(jnp.int32)


def block_scale(own_key, extent, pieces, least, top_value):
    def one(axis_at, shards_of):
        steps = jax.random.uniform(jax.random.fold_in(jax.random.fold_in(own_key, 6), axis_at), (shards_of,), jnp.float32, least / len(pieces), top_value / len(pieces))
        return jnp.repeat(jnp.exp(steps), extent[axis_at] // shards_of).reshape((-1,) + (1,) * (len(extent) - axis_at - 1))

    factor_of = one(*pieces[0])
    for cut in pieces[1:]:
        factor_of = factor_of * one(*cut)
    return factor_of


def centred(stream_key, dims, scale, most, cuts=(), kind=jnp.bfloat16):
    values = jax.random.normal(stream_key, dims, jnp.float32) * scale
    if len(cuts) > 0:
        values = block_scale(stream_key, dims, cuts, -0.22, 0.18) * values
    return jnp.clip(values, min=-most, max=most).astype(kind)


def setup_inputs(seed: int = 0) -> dict:
    seeds = jax.random.split(jax.random.key(seed), 6)
    return {
        "positions": jnp.clip(1.0 * jax.random.uniform(seeds[0], (3, NP), jnp.float32) ** block_scale(seeds[0], (3, NP), ((1, 32),), -0.2, 0.2), 0.0, 1.0),
        "strengths": centred(seeds[1], (3, NP), 0.01, 0.06, ((1, 32),), jnp.float32),
        "radii": jnp.clip(jnp.exp(math.log(0.3) - 1.0986123 * jax.random.uniform(seeds[2], (NP,), jnp.float32) ** block_scale(seeds[2], (NP,), ((0, 32),), -0.2, 0.2)), 0.1, 0.3),
        "pair_list": draw_pair_list(jax.random.fold_in(seeds[5], 71), 0),
        "pair_count": draw_pair_count(jax.random.fold_in(seeds[5], 71), 0),
    }


def cross_rows(u_a, u_b):
    return jnp.stack([u_a[1] * u_b[2] - u_a[2] * u_b[1], u_a[2] * u_b[0] - u_a[0] * u_b[2], u_a[0] * u_b[1] - u_a[1] * u_b[0]])


def pair_terms(pos_a, str_a, rad_a, pos_b, str_b, rad_b):
    rvec = pos_a[:, :, None] - pos_b[:, None, :]
    rho = jnp.sum(rvec * rvec, axis=0)
    spread = 0.5 * (rad_a[:, None] ** 2 + rad_b[None, :] ** 2)
    inner = rho + spread
    power = inner ** -2.5
    upper = rho + 2.5 * spread
    kern = upper * power
    slope = 2.0 * (power - 2.5 * upper * power / inner)
    scale = 1.0 / (4.0 * jnp.pi)
    sa = str_a[:, :, None]
    sb = str_b[:, None, :]
    r_x_b = cross_rows(rvec, sb)
    r_x_a = cross_rows(rvec, sa)
    a_x_b = cross_rows(sa, sb)
    dot_a = jnp.sum(sa * rvec, axis=0)
    dot_b = jnp.sum(sb * rvec, axis=0)
    vel_a = -scale * jnp.sum(kern * r_x_b, axis=2)
    vel_b = scale * jnp.sum(kern * r_x_a, axis=1)
    str_ta = -scale * jnp.sum(kern * a_x_b + slope * dot_a * r_x_b, axis=2)
    str_tb = -scale * jnp.sum(-kern * a_x_b + slope * dot_b * r_x_a, axis=1)
    return jnp.concatenate([vel_a, str_ta]), jnp.concatenate([vel_b, str_tb])


def reference(positions, strengths, radii, pair_list, pair_count):
    rows_i = jnp.arange(N_ROW, dtype=jnp.int32)[:, None, None]
    cols_i = jnp.arange(N_COL, dtype=jnp.int32)[None, :, None]
    slots = jnp.arange(PMAX, dtype=jnp.int32)[None, None, :]
    kk = pair_list[0]
    mm = pair_list[1]
    grp_a = (rows_i * N_COL + kk // GD) * GD + kk % GD
    grp_b = ((mm // GD) * N_COL + cols_i) * GD + mm % GD
    live = (slots < pair_count[:, :, None]).astype(jnp.int32)
    grp_a = grp_a.reshape(-1).astype(jnp.int32)
    grp_b = grp_b.reshape(-1).astype(jnp.int32)
    live = live.reshape(-1)
    total = jnp.zeros((6, positions.shape[1]), jnp.float32)

    def visit(acc, item):
        ga, gb, lv = item

        def work(acc_in):
            sa = (ga * G).astype(jnp.int32)
            sb = (gb * G).astype(jnp.int32)
            pa = lax.dynamic_slice_in_dim(positions, sa, G, 1)
            pb = lax.dynamic_slice_in_dim(positions, sb, G, 1)
            ta = lax.dynamic_slice_in_dim(strengths, sa, G, 1)
            tb = lax.dynamic_slice_in_dim(strengths, sb, G, 1)
            ra = lax.dynamic_slice_in_dim(radii, sa, G, 0)
            rb = lax.dynamic_slice_in_dim(radii, sb, G, 0)
            side_a, side_b = pair_terms(pa, ta, ra, pb, tb, rb)
            other = jnp.where(ga == gb, 0.0, 1.0).astype(jnp.float32)
            cur_a = lax.dynamic_slice_in_dim(acc_in, sa, G, 1)
            acc_in = lax.dynamic_update_slice_in_dim(acc_in, cur_a + side_a, sa, 1)
            cur_b = lax.dynamic_slice_in_dim(acc_in, sb, G, 1)
            return lax.dynamic_update_slice_in_dim(acc_in, cur_b + other * side_b, sb, 1)

        return lax.cond(lv > 0, work, lambda acc_in: acc_in, acc), None

    total, unused = lax.scan(visit, total, (grp_a, grp_b, live))
    return total[:3], total[3:]
```

```python
import functools
import math

import jax
import jax.numpy as jnp
from jax import lax
from jax.experimental import pallas as pl
from jax.experimental.pallas import tpu as pltpu
from jax.sharding import PartitionSpec as P

F32 = jnp.float32
BF16 = jnp.bfloat16
UNIT = 256
STRIP = 16
G_ROWS = 32
H_ROWS = 96
G_SCALE = -1.5 / (4.0 * math.pi)
H_SCALE = 7.5 / (4.0 * math.pi)
VMEM = 48 * 1024 * 1024


def cross(u, v):
    return jnp.concatenate(
        [
            u[1:2] * v[2:3] - u[2:3] * v[1:2],
            u[2:3] * v[0:1] - u[0:1] * v[2:3],
            u[0:1] * v[1:2] - u[1:2] * v[0:1],
        ]
    )


def split(f):
    hi = f.astype(BF16).astype(F32)
    mid = (f - hi).astype(BF16).astype(F32)
    return [hi, mid, (f - hi) - mid]


def features(pack):
    pos = pack[0:3] - 0.5
    st = pack[3:6]
    e0 = jnp.concatenate([st, cross(pos, st), jnp.zeros((2, pack.shape[1]), F32)])
    moments = jnp.concatenate([e0, pos[0:1] * e0, pos[1:2] * e0, pos[2:3] * e0])
    for_g = jnp.concatenate(split(e0) + [jnp.zeros_like(e0)]).astype(BF16)
    return for_g, jnp.concatenate(split(moments)).astype(BF16)


def finish(pack, g, h, code):
    g = g[0:8] + g[8:16] + g[16:24]
    h = h[0:32] + h[32:64] + h[64:96]
    pos = pack[0:3] - 0.5
    st = pack[3:6]
    dot = jnp.sum(pos * st, axis=0, keepdims=True)
    d = dot * h[0:8] - st[0:1] * h[8:16] - st[1:2] * h[16:24] - st[2:3] * h[24:32]
    vel = G_SCALE * (cross(pos, g[0:3]) - g[3:6])
    stretch = G_SCALE * cross(st, g[0:3]) + H_SCALE * (cross(pos, d[0:3]) - d[3:6])
    return jnp.concatenate([vel, stretch, jnp.full((2, pack.shape[1]), code, F32)])


def strip(col, row, images, r):
    ghi, glo, hhi, hlo = images
    here = slice(r, r + STRIP)
    dx = col[:, 0:1] - row[0]
    dy = col[:, 1:2] - row[1]
    dz = col[:, 2:3] - row[2]
    s = col[:, 3:4] + row[3]
    qq = dx * dx + dy * dy + dz * dz + s
    t = lax.rsqrt(qq)
    t2 = t * t
    v = s * t2
    t3 = t2 * t
    g = t3 * (v + 2.0 / 3.0)
    h = (t3 * t2) * (v + 0.4)
    high = g.astype(BF16)
    ghi[here] = high
    glo[here] = (g - high.astype(F32)).astype(BF16)
    high = h.astype(BF16)
    hhi[here] = high
    hlo[here] = (h - high.astype(F32)).astype(BF16)


def down(f, image):
    return jnp.dot(f, image, preferred_element_type=F32)


def across(f, image):
    return lax.dot_general(f, image, (((1,), (1,)), ((), ())), preferred_element_type=F32)


def placed(pack):
    half = 0.5 * pack[6:7] * pack[6:7]
    return jnp.concatenate([pack[0:3], half, jnp.zeros((4, pack.shape[1]), F32)])


def interact(acol, brow, feat_a, slots, sums_b, feat_b=None, sums_a=None):
    for total in sums_b + (sums_a or ()):
        total[...] = jnp.zeros_like(total)

    def products(i, j, images):
        pi, pj = slice(i, i + UNIT), slice(j, j + UNIT)
        steps = []

        def add(total, part, f, form, image):
            total[:, part] += form(f, image[...])

        for n, image in enumerate(images):
            kind = n // 2
            f = feat_a[kind][:, pi]
            steps.append(functools.partial(add, sums_b[kind], pj, f, down, image))
            if sums_a is not None:
                f = feat_b[kind][:, pj]
                steps.append(functools.partial(add, sums_a[kind], pi, f, across, image))
        return steps

    n_strip = UNIT // STRIP
    waiting = []
    count = 0
    for j in range(0, brow.shape[1], UNIT):
        row = [jnp.broadcast_to(brow[n : n + 1, j : j + UNIT], (STRIP, UNIT)) for n in range(4)]
        for i in range(0, acol.shape[0], UNIT):
            images = slots[count % 2]
            count += 1
            per = n_strip // max(1, len(waiting))
            for n in range(n_strip):
                strip(acol[i + n * STRIP : i + (n + 1) * STRIP, :], row, images, n * STRIP)
                if waiting and (n + 1) % per == 0:
                    waiting.pop(0)()
            waiting = products(i, j, images)
    for step in waiting:
        step()


def own_chunk(n, pack, acol, feat, out, brow, sums, slots):
    part = slice(n * out.shape[1], (n + 1) * out.shape[1])
    brow[...] = placed(pack[:, part])
    interact(acol, brow, feat, slots, sums)
    out[...] = finish(pack[:, part], sums[0][...], sums[1][...], 0.0)


def first_kernel(pack, out, acol, feat_g, feat_h, brow, b_g, b_h, *flat):
    acol[...] = jnp.transpose(placed(pack[...]))
    feat_g[...], feat_h[...] = features(pack[...])
    own_chunk(0, pack, acol, (feat_g, feat_h), out, brow, (b_g, b_h), (flat[0:4], flat[4:8]))


def second_kernel(pair_list, pair_count, pack, acol, feat_g, feat_h, after, out, info, brow, b_g, b_h, *flat):
    del after
    k, m = pair_list[0, 0, 0, 1], pair_list[1, 0, 0, 1]
    info[0] = k
    info[1] = m
    info[2] = pair_count[0, 0]
    own_chunk(1, pack, acol, (feat_g, feat_h), out, brow, (b_g, b_h), (flat[0:4], flat[4:8]))


def later_kernel(n, pack, acol, feat_g, feat_h, after, out, brow, b_g, b_h, *flat):
    del after
    own_chunk(n, pack, acol, (feat_g, feat_h), out, brow, (b_g, b_h), (flat[0:4], flat[4:8]))


def pack_kernel(positions, strengths, radii, pack, sems):
    copies = [
        pltpu.make_async_copy(positions, pack.at[0:3], sems.at[0]),
        pltpu.make_async_copy(strengths, pack.at[3:6], sems.at[1]),
        pltpu.make_async_copy(radii, pack.at[6:7], sems.at[2]),
    ]
    for copy in copies:
        copy.start()
    for copy in copies:
        copy.wait()


def here(axis):
    return lax.axis_index(axis).astype(jnp.int32)


def choose(relative, near, far):
    at = relative // 2
    return jnp.where(relative % 2 == 0, near[at], far[at])


def stack_kernel(n_a, after, *refs):
    del after
    blocks_a, blocks_b, (near_a, near_b) = refs[:n_a], refs[n_a:-2], refs[-2:]
    for blocks, near in ((blocks_a, near_a), (blocks_b, near_b)):
        for n, block in enumerate(blocks):
            near[n] = block[...]


def pair_kernel(info, near_a, far_a, near_b, far_b, after, out_a, out_b, apack, bpack, acol, brow, *rest):
    del after
    sums_b, sums_a, slots = rest[0:2], rest[2:4], (rest[4:8], rest[8:12])
    blank = jnp.full((2, out_a.shape[1]), -1.0, F32)
    out_a[6:8] = blank
    out_b[6:8] = blank

    @pl.when(info[2] > 1)
    def _():
        k = info[0]
        m = info[1]
        from_a = k ^ here("col")
        from_b = m ^ here("row")
        apack[...] = choose(from_a, near_a, far_a)
        bpack[...] = choose(from_b, near_b, far_b)
        acol[...] = jnp.transpose(placed(apack[...]))
        brow[...] = placed(bpack[...])
        feat_a, feat_b = features(apack[...]), features(bpack[...])
        interact(acol, brow, feat_a, slots, sums_b, feat_b, sums_a)
        out_a[...] = finish(apack[...], sums_a[0][...], sums_a[1][...], k.astype(F32))

        @pl.when((from_a | from_b) != 0)
        def _():
            out_b[...] = finish(bpack[...], sums_b[0][...], sums_b[1][...], m.astype(F32))


def merge_kernel(n_a, after, *refs):
    del after
    parts_a, parts_b, (keep, send_a, send_b) = refs[:n_a], refs[n_a:-3], refs[-3:]
    total = jnp.zeros(keep.shape, F32)
    for axis, parts, send in (("col", parts_a, send_a), ("row", parts_b, send_b)):
        at = here(axis)
        onward = jnp.zeros_like(total)
        for part in parts:
            block = part[...]
            total += jnp.where(block[6:7] == at.astype(F32), block, 0.0)
            onward += jnp.where(block[6:7] == (at ^ 1).astype(F32), block, 0.0)
        send[...] = onward
    keep[...] = total


def sum_kernel(keep, part_a, part_b, *refs):
    own, (velocity, stretching) = refs[:-2], refs[-2:]
    total = keep[...] + part_a[...] + part_b[...]
    total += jnp.concatenate([chunk[...] for chunk in own], axis=1)
    velocity[...] = total[0:3]
    stretching[...] = total[3:6]


def work(cols, rows, sides):
    images = [pltpu.VMEM((UNIT, UNIT), BF16)] * 8
    sums_b = [pltpu.VMEM((G_ROWS, cols), F32), pltpu.VMEM((H_ROWS, cols), F32)]
    sums_a = [pltpu.VMEM((G_ROWS, rows), F32), pltpu.VMEM((H_ROWS, rows), F32)]
    return [pltpu.VMEM((8, cols), F32)] + sums_b + sums_a * (sides - 1) + images


def swap(block, axis, size, step):
    return lax.ppermute(block, axis, [(i, i ^ step) for i in range(size)])


def spread(block, axis, size):
    return [block] + [swap(block, axis, size, 2 * s) for s in range(1, size // 2)]


def local(n_row, n_col, positions, strengths, radii, pair_list, pair_count):
    g = radii.shape[0]
    part = g // 4
    hbm_spec = pl.BlockSpec(memory_space=pltpu.HBM)
    vmem_spec = pl.BlockSpec(memory_space=pltpu.VMEM)
    smem_spec = pl.BlockSpec(memory_space=pltpu.SMEM)
    params = pltpu.CompilerParams(vmem_limit_bytes=VMEM)
    block = jax.ShapeDtypeStruct((8, g), F32)
    chunk = jax.ShapeDtypeStruct((8, part), F32)
    chunk_cost = pl.CostEstimate(flops=30 * g * part, bytes_accessed=64 * g, transcendentals=g * part)
    chunk_call = functools.partial(
        pl.pallas_call, scratch_shapes=work(part, g, 1), compiler_params=params, cost_estimate=chunk_cost
    )

    pack = pl.pallas_call(
        pack_kernel,
        out_shape=block,
        in_specs=[hbm_spec] * 3,
        out_specs=vmem_spec,
        scratch_shapes=[pltpu.SemaphoreType.DMA((3,))],
        name="pack_group",
    )(positions, strengths, radii[None])

    blocks_a = spread(pack, "col", n_col)
    blocks_b = spread(pack, "row", n_row)
    own_0, *common = chunk_call(
        first_kernel,
        out_shape=(
            chunk,
            jax.ShapeDtypeStruct((g, 8), F32),
            jax.ShapeDtypeStruct((G_ROWS, g), BF16),
            jax.ShapeDtypeStruct((H_ROWS, g), BF16),
        ),
        in_specs=[vmem_spec],
        out_specs=(vmem_spec,) * 4,
        name="own_first",
    )(pack)
    near_a, near_b = pl.pallas_call(
        functools.partial(stack_kernel, len(blocks_a)),
        out_shape=(
            jax.ShapeDtypeStruct((len(blocks_a), 8, g), F32),
            jax.ShapeDtypeStruct((len(blocks_b), 8, g), F32),
        ),
        in_specs=[vmem_spec] * (1 + len(blocks_a) + len(blocks_b)),
        out_specs=(vmem_spec,) * 2,
        compiler_params=params,
        name="stack_groups",
    )(own_0, *blocks_a, *blocks_b)

    far_a = swap(near_a, "col", n_col, 1)
    far_b = swap(near_b, "row", n_row, 1)
    own_1, info = chunk_call(
        second_kernel,
        out_shape=(chunk, jax.ShapeDtypeStruct((3,), jnp.int32)),
        in_specs=[smem_spec] * 2 + [vmem_spec] * 5,
        out_specs=(vmem_spec, smem_spec),
        name="own_second",
    )(pair_list, pair_count, pack, *common, near_b)

    side_a, side_b = pl.pallas_call(
        pair_kernel,
        out_shape=(block, block),
        in_specs=[smem_spec] + [vmem_spec] * 5,
        out_specs=(vmem_spec, vmem_spec),
        scratch_shapes=[pltpu.VMEM((8, g), F32)] * 2 + [pltpu.VMEM((g, 8), F32)] + work(g, g, 2),
        compiler_params=params,
        cost_estimate=pl.CostEstimate(flops=60 * g * g, bytes_accessed=128 * g, transcendentals=g * g),
        name="listed_pair",
    )(info, near_a, far_a, near_b, far_b, own_1)

    parts_a = spread(side_a, "col", n_col)
    parts_b = spread(side_b, "row", n_row)
    own_2 = chunk_call(
        functools.partial(later_kernel, 2),
        out_shape=chunk,
        in_specs=[vmem_spec] * 5,
        out_specs=vmem_spec,
        name="own_third",
    )(pack, *common, side_b)
    keep, send_a, send_b = pl.pallas_call(
        functools.partial(merge_kernel, len(parts_a)),
        out_shape=(block,) * 3,
        in_specs=[vmem_spec] * (1 + len(parts_a) + len(parts_b)),
        out_specs=(vmem_spec,) * 3,
        compiler_params=params,
        name="merge_parts",
    )(own_2, *parts_a, *parts_b)

    far_a = swap(send_a, "col", n_col, 1)
    far_b = swap(send_b, "row", n_row, 1)
    own_3 = chunk_call(
        functools.partial(later_kernel, 3),
        out_shape=chunk,
        in_specs=[vmem_spec] * 5,
        out_specs=vmem_spec,
        name="own_fourth",
    )(pack, *common, keep)

    three = jax.ShapeDtypeStruct((3, g), F32)
    return pl.pallas_call(
        sum_kernel,
        out_shape=(three, three),
        in_specs=[vmem_spec] * 7,
        out_specs=(vmem_spec, vmem_spec),
        compiler_params=params,
        name="sum_parts",
    )(keep, far_a, far_b, own_0, own_1, own_2, own_3)


def solution(mesh):
    placed = (
        P(None, ("row", "col")),
        P(None, ("row", "col")),
        P(("row", "col")),
        P(None, "row", "col", None),
        P("row", "col"),
    )
    return jax.shard_map(
        functools.partial(local, mesh.shape["row"], mesh.shape["col"]),
        mesh=mesh,
        in_specs=placed,
        out_specs=(P(None, ("row", "col")), P(None, ("row", "col"))),
        check_vma=False,
    )
```

```python
import functools
import math

import jax
import jax.numpy as jnp
from jax import lax
from jax.experimental import pallas as pl
from jax.experimental.pallas import tpu as pltpu
from jax.sharding import PartitionSpec as P

F32 = jnp.float32
BF16 = jnp.bfloat16
UNIT = 256
STRIP = 16
G_ROWS = 32
H_ROWS = 96
Q_ROWS = 32
G_SCALE = -1.5 / (4.0 * math.pi)
H_SCALE = 7.5 / (4.0 * math.pi)
VMEM = 48 * 1024 * 1024


def cross(u, v):
    return jnp.concatenate(
        [
            u[1:2] * v[2:3] - u[2:3] * v[1:2],
            u[2:3] * v[0:1] - u[0:1] * v[2:3],
            u[0:1] * v[1:2] - u[1:2] * v[0:1],
        ]
    )


def split(f):
    hi = f.astype(BF16).astype(F32)
    mid = (f - hi).astype(BF16).astype(F32)
    return [hi, mid, (f - hi) - mid]


def features(pack):
    pos = pack[0:3] - 0.5
    st = pack[3:6]
    e0 = jnp.concatenate([st, cross(pos, st), jnp.zeros((2, pack.shape[1]), F32)])
    moments = jnp.concatenate([e0, pos[0:1] * e0, pos[1:2] * e0, pos[2:3] * e0])
    for_g = jnp.concatenate(split(e0) + [jnp.zeros_like(e0)]).astype(BF16)
    return for_g, jnp.concatenate(split(moments)).astype(BF16)


def widen(pack, wide):
    for_g, for_h = features(pack)
    both = jnp.transpose(jnp.concatenate([for_h, for_g]).astype(F32)).astype(BF16)
    at = lax.broadcasted_iota(jnp.int32, both.shape, 1)
    wide[0][...] = jnp.where(at < H_ROWS, 0.0, both.astype(F32)).astype(BF16)
    wide[1][...] = jnp.where(at < H_ROWS, both.astype(F32), 0.0).astype(BF16)


def finish(pack, g, h, code):
    g = g[0:8] + g[8:16] + g[16:24]
    h = h[0:32] + h[32:64] + h[64:96]
    pos = pack[0:3] - 0.5
    st = pack[3:6]
    dot = jnp.sum(pos * st, axis=0, keepdims=True)
    d = dot * h[0:8] - st[0:1] * h[8:16] - st[1:2] * h[16:24] - st[2:3] * h[24:32]
    vel = G_SCALE * (cross(pos, g[0:3]) - g[3:6])
    stretch = G_SCALE * cross(st, g[0:3]) + H_SCALE * (cross(pos, d[0:3]) - d[3:6])
    return jnp.concatenate([vel, stretch, jnp.full((2, pack.shape[1]), code, F32)])


def strip(qq, s, images, r):
    ghi, glo, hhi, hlo = images
    here = slice(r, r + STRIP)
    t = lax.rsqrt(qq)
    t2 = t * t
    v = s * t2
    t3 = t2 * t
    g = t3 * (v + 2.0 / 3.0)
    h = (t3 * t2) * (v + 0.4)
    high = g.astype(BF16)
    ghi[here] = high
    glo[here] = (g - high.astype(F32)).astype(BF16)
    high = h.astype(BF16)
    hhi[here] = high
    hlo[here] = (h - high.astype(F32)).astype(BF16)


def down(f, image):
    return jnp.dot(f, image, preferred_element_type=F32)


def halves(pack):
    return 0.5 * pack[6:7] * pack[6:7]


def distances(pack):
    pos = pack[0:3] - 0.5
    x1, x2, x3 = split(pos)
    norm = jnp.concatenate(split(jnp.sum(pos * pos, axis=0, keepdims=True) + halves(pack)))
    one = jnp.ones_like(norm)
    blank = jnp.zeros((8, pack.shape[1]), F32)
    left = [-2.0 * x for x in (x1, x1, x2, x2, x1, x3)] + [norm, one, blank]
    right = [x1, x2, x1, x2, x3, x1, one, norm, blank]
    return jnp.concatenate(left), jnp.concatenate(right).astype(BF16)


def columns(pack, dist, spread_s):
    left, right = distances(pack)
    dist[...] = jnp.transpose(left).astype(BF16)
    spread_s[...] = jnp.transpose(jnp.broadcast_to(halves(pack), (8, pack.shape[1])))
    return right


def interact(dist_a, s_a, dist_b, s_b, feat_a, qq, slots, sums_b):
    for total in sums_b:
        total[...] = jnp.zeros_like(total)

    def products(i, j, images):
        pi, pj = slice(i, i + UNIT), slice(j, j + UNIT)
        steps = []

        def add(total, f, high, low):
            total[:, pj] += down(f, high[...]) + down(f, low[...])

        for kind in range(2):
            f = feat_a[kind][:, pi]
            steps.append(functools.partial(add, sums_b[kind], f, *images[2 * kind : 2 * kind + 2]))
        return steps

    def measure(unit, into):
        i, j = unit
        into[...] = down(dist_a[i : i + UNIT, :], dist_b[:, j : j + UNIT])

    n_strip = UNIT // STRIP
    units = [(i, j) for j in range(0, s_b.shape[1], UNIT) for i in range(0, s_a.shape[0], UNIT)]
    measure(units[0], qq[0])
    waiting = []
    for count, (i, j) in enumerate(units):
        images = slots[count % 2]
        if count + 1 < len(units):
            waiting.insert(0, functools.partial(measure, units[count + 1], qq[(count + 1) % 2]))
        per = n_strip // max(1, len(waiting))
        row = jnp.broadcast_to(s_b[0:1, j : j + UNIT], (STRIP, UNIT))
        for n in range(n_strip):
            at = slice(i + n * STRIP, i + (n + 1) * STRIP)
            here = slice(n * STRIP, (n + 1) * STRIP)
            strip(qq[count % 2][here, :], s_a[at, 0:1] + row, images, n * STRIP)
            if waiting and (n + 1) % per == 0:
                waiting.pop(0)()
        for step in waiting:
            step()
        waiting = products(i, j, images)
    for step in waiting:
        step()


def interact_both(dist_a, s_a, dist_b, s_b, feat_a, wide_b, qq, images, acc, sums_b):
    rows, n = s_a.shape[0], UNIT
    blocks = s_b.shape[1] // n

    def measure(block):
        part = slice(block * n, (block + 1) * n)
        for i in range(0, rows, n):
            qq[block % 2][i : i + n, :] = down(dist_a[i : i + n, :], dist_b[:, part])

    def onto_a(block, i):
        here, part = slice(i, i + n), slice(block * n, (block + 1) * n)
        wide = jnp.concatenate([wide_b[0][part, :]] * 2 + [wide_b[1][part, :]] * 2)
        share = down(images[block % 2][here, :], wide)
        acc[here, :] = share if block == 0 else acc[here, :] + share

    def onto_b(block, kind):
        part = slice(block * n, (block + 1) * n)
        image = images[block % 2]
        at = 2 * kind * n
        total = down(feat_a[kind], image[:, at : at + n])
        sums_b[kind][:, part] = total + down(feat_a[kind], image[:, at + n : at + 2 * n])

    measure(0)
    waiting = []
    for block in range(blocks):
        image = images[block % 2]
        part = slice(block * n, (block + 1) * n)
        slots = [image.at[:, m * n : (m + 1) * n] for m in range(4)]
        row = jnp.broadcast_to(s_b[0:1, part], (STRIP, n))
        if block + 1 < blocks:
            waiting.append(functools.partial(measure, block + 1))
        n_strip = rows // STRIP
        per = max(1, n_strip // max(1, len(waiting)))
        for m in range(n_strip):
            here = slice(m * STRIP, (m + 1) * STRIP)
            strip(qq[block % 2][here, :], s_a[here, 0:1] + row, slots, m * STRIP)
            if waiting and (m + 1) % per == 0:
                waiting.pop(0)()
        for step in waiting:
            step()
        waiting = []
        for m, i in enumerate(range(0, rows, n)):
            waiting.append(functools.partial(onto_a, block, i))
            if m % 2 == 1 and m // 2 < 2:
                waiting.append(functools.partial(onto_b, block, 1 - m // 2))
    for step in waiting:
        step()


def own_chunk(n, pack, dist, s_col, right, feat, out, sums, qq, slots):
    part = slice(n * out.shape[1], (n + 1) * out.shape[1])
    interact(dist, s_col, right[:, part], halves(pack[:, part]), feat, qq, slots, sums)
    out[...] = finish(pack[:, part], sums[0][...], sums[1][...], 0.0)


def first_kernel(pack, after, out, dist, s_col, right, feat_g, feat_h, b_g, b_h, *flat):
    del after
    right[...] = columns(pack[...], dist, s_col)
    feat_g[...], feat_h[...] = features(pack[...])
    own_chunk(0, pack, dist, s_col, right, (feat_g, feat_h), out, (b_g, b_h), flat[0:2], (flat[2:6], flat[6:10]))


def later_kernel(n, pack, dist, s_col, right, feat_g, feat_h, after, out, b_g, b_h, *flat):
    del after
    own_chunk(n, pack, dist, s_col, right, (feat_g, feat_h), out, (b_g, b_h), flat[0:2], (flat[2:6], flat[6:10]))


def pack_kernel(positions, strengths, radii, pair_list, pair_count, pack, listed, count, sems):
    copies = [
        pltpu.make_async_copy(pair_list, listed, sems.at[0]),
        pltpu.make_async_copy(pair_count, count, sems.at[1]),
        pltpu.make_async_copy(positions, pack.at[0:3], sems.at[2]),
        pltpu.make_async_copy(strengths, pack.at[3:6], sems.at[3]),
        pltpu.make_async_copy(radii, pack.at[6:7], sems.at[4]),
    ]
    for copy in copies:
        copy.start()
    for copy in copies[:2]:
        copy.wait()
    for n, value in enumerate((listed[0, 0, 0, 1], listed[1, 0, 0, 1], count[0, 0])):
        pack[7:8, n * 128 : (n + 1) * 128] = jnp.full((1, 128), value.astype(F32))
    rest = pack.shape[1] - 3 * 128
    pack[7:8, 3 * 128 :] = jnp.zeros((1, rest), F32)
    for copy in copies[2:]:
        copy.wait()


def here(axis):
    return lax.axis_index(axis).astype(jnp.int32)


def choose(relative, near, far):
    at = relative // 2
    return jnp.where(relative % 2 == 0, near[at], far[at])


def stack_kernel(after, *refs):
    del after
    blocks, near = refs[:-1], refs[-1]
    for n, block in enumerate(blocks):
        near[n] = block[...]


def pair_kernel(pack, near_a, far_a, near_b, far_b, after, out_a, out_b, apack, bpack, dist, s_col, *rest):
    del after
    sums_b, wide_b, qq, images, acc = rest[0:2], rest[2:4], rest[4:6], rest[6:8], rest[8]
    k, m, count = [jnp.max(pack[7:8, n * 128 : (n + 1) * 128]).astype(jnp.int32) for n in range(3)]
    blank = jnp.full((2, out_a.shape[1]), -1.0, F32)
    out_a[6:8] = blank
    out_b[6:8] = blank

    @pl.when(count > 1)
    def _():
        from_a = k ^ here("col")
        from_b = m ^ here("row")
        apack[...] = choose(from_a, near_a, far_a)
        bpack[...] = choose(from_b, near_b, far_b)
        columns(apack[...], dist, s_col)
        right = distances(bpack[...])[1]
        widen(bpack[...], wide_b)
        feat_a = features(apack[...])
        interact_both(dist, s_col, right, halves(bpack[...]), feat_a, wide_b, qq, images, acc, sums_b)
        total = jnp.transpose(acc[...])
        out_a[...] = finish(apack[...], total[H_ROWS:], total[:H_ROWS], k.astype(F32))

        @pl.when((from_a | from_b) != 0)
        def _():
            out_b[...] = finish(bpack[...], sums_b[0][...], sums_b[1][...], m.astype(F32))


def merge_kernel(axis, after, *refs):
    del after
    parts, (keep, send) = refs[:-2], refs[-2:]
    at = here(axis)
    total = onward = jnp.zeros(keep.shape, F32)
    for part in parts:
        block = part[...]
        total += jnp.where(block[6:7] == at.astype(F32), block, 0.0)
        onward += jnp.where(block[6:7] == (at ^ 1).astype(F32), block, 0.0)
    keep[...] = total
    send[...] = onward


def sum_kernel(keep_a, keep_b, part_a, part_b, *refs):
    own, (velocity, stretching) = refs[:-2], refs[-2:]
    total = keep_a[...] + keep_b[...] + part_a[...] + part_b[...]
    total += jnp.concatenate([chunk[...] for chunk in own], axis=1)
    velocity[...] = total[0:3]
    stretching[...] = total[3:6]


def own_work(cols):
    return [
        pltpu.VMEM((G_ROWS, cols), F32),
        pltpu.VMEM((H_ROWS, cols), F32),
        *[pltpu.VMEM((UNIT, UNIT), F32)] * 2,
        *[pltpu.VMEM((UNIT, UNIT), BF16)] * 8,
    ]


def pair_work(g):
    return [
        *[pltpu.VMEM((8, g), F32)] * 2,
        pltpu.VMEM((g, Q_ROWS), BF16),
        pltpu.VMEM((g, 8), F32),
        pltpu.VMEM((G_ROWS, g), F32),
        pltpu.VMEM((H_ROWS, g), F32),
        *[pltpu.VMEM((g, G_ROWS + H_ROWS), BF16)] * 2,
        *[pltpu.VMEM((g, UNIT), F32)] * 2,
        *[pltpu.VMEM((g, 4 * UNIT), BF16)] * 2,
        pltpu.VMEM((g, G_ROWS + H_ROWS), F32),
    ]


def swap(block, axis, size, step):
    return lax.ppermute(block, axis, [(i, i ^ step) for i in range(size)])


def spread(block, axis, size):
    return [block] + [swap(block, axis, size, 2 * s) for s in range(1, size // 2)]


def local(n_row, n_col, positions, strengths, radii, pair_list, pair_count):
    g = radii.shape[0]
    part = g // 4
    hbm_spec = pl.BlockSpec(memory_space=pltpu.HBM)
    vmem_spec = pl.BlockSpec(memory_space=pltpu.VMEM)
    params = pltpu.CompilerParams(vmem_limit_bytes=VMEM)
    block = jax.ShapeDtypeStruct((8, g), F32)
    chunk = jax.ShapeDtypeStruct((8, part), F32)
    chunk_cost = pl.CostEstimate(flops=30 * g * part, bytes_accessed=64 * g, transcendentals=g * part)
    chunk_call = functools.partial(
        pl.pallas_call, scratch_shapes=own_work(part), compiler_params=params, cost_estimate=chunk_cost
    )

    pack = pl.pallas_call(
        pack_kernel,
        out_shape=block,
        in_specs=[hbm_spec] * 5,
        out_specs=vmem_spec,
        scratch_shapes=[
            pltpu.SMEM(pair_list.shape, jnp.int32),
            pltpu.SMEM(pair_count.shape, jnp.int32),
            pltpu.SemaphoreType.DMA((5,)),
        ],
        compiler_params=params,
        name="pack_group",
    )(positions, strengths, radii[None], pair_list, pair_count)

    blocks_a = spread(pack, "col", n_col)
    blocks_b = spread(pack, "row", n_row)
    def stack(after, blocks, name):
        return pl.pallas_call(
            stack_kernel,
            out_shape=jax.ShapeDtypeStruct((len(blocks), 8, g), F32),
            in_specs=[vmem_spec] * (1 + len(blocks)),
            out_specs=vmem_spec,
            compiler_params=params,
            name=name,
        )(after, *blocks)

    near_b = stack(pack, blocks_b, "stack_row")
    far_b = swap(near_b, "row", n_row, 1)
    own_0, *common = chunk_call(
        first_kernel,
        out_shape=(
            chunk,
            jax.ShapeDtypeStruct((g, Q_ROWS), BF16),
            jax.ShapeDtypeStruct((g, 8), F32),
            jax.ShapeDtypeStruct((Q_ROWS, g), BF16),
            jax.ShapeDtypeStruct((G_ROWS, g), BF16),
            jax.ShapeDtypeStruct((H_ROWS, g), BF16),
        ),
        in_specs=[vmem_spec] * 2,
        out_specs=(vmem_spec,) * 6,
        name="own_first",
    )(pack, near_b)
    near_a = stack(own_0, blocks_a, "stack_col")
    far_a = swap(near_a, "col", n_col, 1)
    own_1 = chunk_call(
        functools.partial(later_kernel, 1),
        out_shape=chunk,
        in_specs=[vmem_spec] * 7,
        out_specs=vmem_spec,
        name="own_second",
    )(pack, *common, near_a)

    side_a, side_b = pl.pallas_call(
        pair_kernel,
        out_shape=(block, block),
        in_specs=[vmem_spec] * 6,
        out_specs=(vmem_spec, vmem_spec),
        scratch_shapes=pair_work(g),
        compiler_params=params,
        cost_estimate=pl.CostEstimate(flops=60 * g * g, bytes_accessed=128 * g, transcendentals=g * g),
        name="listed_pair",
    )(pack, near_a, far_a, near_b, far_b, own_1)

    parts_a = spread(side_a, "col", n_col)
    parts_b = spread(side_b, "row", n_row)
    own_2 = chunk_call(
        functools.partial(later_kernel, 2),
        out_shape=chunk,
        in_specs=[vmem_spec] * 7,
        out_specs=vmem_spec,
        name="own_third",
    )(pack, *common, side_b)
    def merge(after, parts, axis):
        return pl.pallas_call(
            functools.partial(merge_kernel, axis),
            out_shape=(block,) * 2,
            in_specs=[vmem_spec] * (1 + len(parts)),
            out_specs=(vmem_spec,) * 2,
            compiler_params=params,
            name="merge_" + axis,
        )(after, *parts)

    keep_b, send_b = merge(pack, parts_b, "row")
    far_b = swap(send_b, "row", n_row, 1)
    keep_a, send_a = merge(own_2, parts_a, "col")
    far_a = swap(send_a, "col", n_col, 1)
    own_3 = chunk_call(
        functools.partial(later_kernel, 3),
        out_shape=chunk,
        in_specs=[vmem_spec] * 7,
        out_specs=vmem_spec,
        name="own_fourth",
    )(pack, *common, keep_a)

    three = jax.ShapeDtypeStruct((3, g), F32)
    return pl.pallas_call(
        sum_kernel,
        out_shape=(three, three),
        in_specs=[vmem_spec] * 8,
        out_specs=(vmem_spec, vmem_spec),
        compiler_params=params,
        name="sum_parts",
    )(keep_a, keep_b, far_a, far_b, own_0, own_1, own_2, own_3)


def solution(mesh):
    placed = (
        P(None, ("row", "col")),
        P(None, ("row", "col")),
        P(("row", "col")),
        P(None, "row", "col", None),
        P("row", "col"),
    )
    return jax.shard_map(
        functools.partial(local, mesh.shape["row"], mesh.shape["col"]),
        mesh=mesh,
        in_specs=placed,
        out_specs=(P(None, ("row", "col")), P(None, ("row", "col"))),
        check_vma=False,
    )
```

```python
import functools
import math

import jax
import jax.numpy as jnp
from jax import lax
from jax.experimental import pallas as pl
from jax.experimental.pallas import tpu as pltpu
from jax.sharding import PartitionSpec as P

F32 = jnp.float32
BF16 = jnp.bfloat16
UNIT = 256
STRIP = 16
G_ROWS = 32
H_ROWS = 96
Q_ROWS = 32
G_SCALE = -1.5 / (4.0 * math.pi)
H_SCALE = 7.5 / (4.0 * math.pi)
VMEM = 48 * 1024 * 1024


def cross(u, v):
    return jnp.concatenate(
        [
            u[1:2] * v[2:3] - u[2:3] * v[1:2],
            u[2:3] * v[0:1] - u[0:1] * v[2:3],
            u[0:1] * v[1:2] - u[1:2] * v[0:1],
        ]
    )


def split(f):
    hi = f.astype(BF16).astype(F32)
    mid = (f - hi).astype(BF16).astype(F32)
    return [hi, mid, (f - hi) - mid]


def features(pack):
    pos = pack[0:3] - 0.5
    st = pack[3:6]
    e0 = jnp.concatenate([st, cross(pos, st), jnp.zeros((2, pack.shape[1]), F32)])
    moments = jnp.concatenate([e0, pos[0:1] * e0, pos[1:2] * e0, pos[2:3] * e0])
    for_g = jnp.concatenate(split(e0) + [jnp.zeros_like(e0)]).astype(BF16)
    return for_g, jnp.concatenate(split(moments)).astype(BF16)


def finish(pack, g, h):
    g = g[0:8] + g[8:16] + g[16:24]
    h = h[0:32] + h[32:64] + h[64:96]
    pos = pack[0:3] - 0.5
    st = pack[3:6]
    dot = jnp.sum(pos * st, axis=0, keepdims=True)
    d = dot * h[0:8] - st[0:1] * h[8:16] - st[1:2] * h[16:24] - st[2:3] * h[24:32]
    vel = G_SCALE * (cross(pos, g[0:3]) - g[3:6])
    stretch = G_SCALE * cross(st, g[0:3]) + H_SCALE * (cross(pos, d[0:3]) - d[3:6])
    return jnp.concatenate([vel, stretch])


def store_dense(out, value):
    rows = value.shape[0]
    for n in range(value.shape[1] // 128):
        out[n * rows : (n + 1) * rows, :] = value[:, n * 128 : (n + 1) * 128]


def load_dense(value, rows):
    return jnp.concatenate([value[n : n + rows] for n in range(0, value.shape[0], rows)], axis=1)


def strip(qq, s, images, r):
    ghi, glo, hhi, hlo = images
    here = slice(r, r + STRIP)
    t = lax.rsqrt(qq)
    t2 = t * t
    v = s * t2
    t3 = t2 * t
    g = t3 * (v + 2.0 / 3.0)
    h = (t3 * t2) * (v + 0.4)
    high = g.astype(BF16)
    ghi[here] = high
    glo[here] = (g - high.astype(F32)).astype(BF16)
    high = h.astype(BF16)
    hhi[here] = high
    hlo[here] = (h - high.astype(F32)).astype(BF16)


def down(f, image):
    return jnp.dot(f, image, preferred_element_type=F32)


def across(f, image):
    return lax.dot_general(f, image, (((1,), (1,)), ((), ())), preferred_element_type=F32)


def halves(pack):
    return 0.5 * pack[6:7] * pack[6:7]


def distances(pack):
    pos = pack[0:3] - 0.5
    x1, x2, x3 = split(pos)
    norm = jnp.concatenate(split(jnp.sum(pos * pos, axis=0, keepdims=True) + halves(pack)))
    one = jnp.ones_like(norm)
    blank = jnp.zeros((8, pack.shape[1]), F32)
    left = [-2.0 * x for x in (x1, x1, x2, x2, x1, x3)] + [norm, one, blank]
    right = [x1, x2, x1, x2, x3, x1, one, norm, blank]
    return jnp.concatenate(left), jnp.concatenate(right).astype(BF16)


def columns(pack, dist, spread_s):
    left, right = distances(pack)
    dist[...] = jnp.transpose(left).astype(BF16)
    spread_s[...] = jnp.transpose(jnp.broadcast_to(halves(pack), (8, pack.shape[1])))
    return right


def interact(dist_a, s_a, dist_b, s_b, feat_a, qq, slots, sums_b):
    for total in sums_b:
        total[...] = jnp.zeros_like(total)

    def products(i, j, images):
        pi, pj = slice(i, i + UNIT), slice(j, j + UNIT)
        steps = []

        def add(total, f, high, low):
            total[:, pj] += down(f, high[...]) + down(f, low[...])

        for kind in range(2):
            f = feat_a[kind][:, pi]
            steps.append(functools.partial(add, sums_b[kind], f, *images[2 * kind : 2 * kind + 2]))
        return steps

    def measure(unit, into):
        i, j = unit
        into[...] = down(dist_a[i : i + UNIT, :], dist_b[:, j : j + UNIT])

    n_strip = UNIT // STRIP
    units = [(i, j) for j in range(0, s_b.shape[1], UNIT) for i in range(0, s_a.shape[0], UNIT)]
    measure(units[0], qq[0])
    waiting = []
    for count, (i, j) in enumerate(units):
        images = slots[count % 2]
        if count + 1 < len(units):
            waiting.insert(0, functools.partial(measure, units[count + 1], qq[(count + 1) % 2]))
        per = n_strip // max(1, len(waiting))
        row = jnp.broadcast_to(s_b[0:1, j : j + UNIT], (STRIP, UNIT))
        for n in range(n_strip):
            at = slice(i + n * STRIP, i + (n + 1) * STRIP)
            here = slice(n * STRIP, (n + 1) * STRIP)
            strip(qq[count % 2][here, :], s_a[at, 0:1] + row, images, n * STRIP)
            if waiting and (n + 1) % per == 0:
                waiting.pop(0)()
        for step in waiting:
            step()
        waiting = products(i, j, images)
    for step in waiting:
        step()


def interact_both(dist_a, s_a, dist_b, s_b, feat_a, feat_b, qq, images, sums_a, sums_b):
    rows, n = s_a.shape[0], UNIT
    blocks, chunks = s_b.shape[1] // n, rows // n
    half = rows // 2

    def measure(block, c):
        here, part = slice(c * n, (c + 1) * n), slice(block * n, (block + 1) * n)
        qq[block % 2][here, :] = down(dist_a[here, :], dist_b[:, part])

    def onto_a(block, c, kind):
        here, part = slice(c * n, (c + 1) * n), slice(block * n, (block + 1) * n)
        f = jnp.concatenate([feat_b[kind][:, part]] * 2, axis=1)
        share = across(f, images[block % 2][here, 2 * kind * n : 2 * (kind + 1) * n])
        sums_a[kind][:, here] = share if block == 0 else sums_a[kind][:, here] + share

    def onto_b(block, later, kind):
        here, part = slice(later * half, (later + 1) * half), slice(block * n, (block + 1) * n)
        image = images[block % 2]
        at = 2 * kind * n
        f = feat_a[kind][:, here]
        share = down(f, image[here, at : at + n]) + down(f, image[here, at + n : at + 2 * n])
        sums_b[kind][:, part] = sums_b[kind][:, part] + share if later else share

    for c in range(chunks):
        measure(0, c)
    ready, delayed = [], []
    for block in range(blocks):
        image = images[block % 2]
        part = slice(block * n, (block + 1) * n)
        slots = [image.at[:, m * n : (m + 1) * n] for m in range(4)]
        row = jnp.broadcast_to(s_b[0:1, part], (STRIP, n))
        for c in range(chunks):
            todo, ready, delayed = ready, delayed, []
            if block + 1 < blocks:
                todo.append(functools.partial(measure, block + 1, c))
            n_strip = n // STRIP
            per = max(1, n_strip // max(1, len(todo)))
            for m in range(n_strip):
                here = slice(c * n + m * STRIP, c * n + (m + 1) * STRIP)
                strip(qq[block % 2][here, :], s_a[here, 0:1] + row, slots, c * n + m * STRIP)
                if todo and (m + 1) % per == 0:
                    todo.pop(0)()
            for step in todo:
                step()
            for kind in range(2):
                ready.append(functools.partial(onto_a, block, c, kind))
            if (c + 1) % (chunks // 2) == 0:
                later = (c + 1) // (chunks // 2) - 1
                ready.append(functools.partial(onto_b, block, later, 0))
                delayed.append(functools.partial(onto_b, block, later, 1))
    for step in ready + delayed:
        step()


def own_chunk(n, pack, dist, s_col, right, feat, out, sums, qq, slots):
    part = slice(n * out.shape[1], (n + 1) * out.shape[1])
    interact(dist, s_col, right[:, part], halves(pack[:, part]), feat, qq, slots, sums)
    out[...] = finish(pack[:, part], sums[0][...], sums[1][...])


def first_kernel(pack, out, dist, s_col, right, feat_g, feat_h, b_g, b_h, *flat):
    right[...] = columns(pack[...], dist, s_col)
    feat_g[...], feat_h[...] = features(pack[...])
    own_chunk(0, pack, dist, s_col, right, (feat_g, feat_h), out, (b_g, b_h), flat[0:2], (flat[2:6], flat[6:10]))


def later_kernel(n, pack, dist, s_col, right, feat_g, feat_h, after, out, b_g, b_h, *flat):
    del after
    own_chunk(n, pack, dist, s_col, right, (feat_g, feat_h), out, (b_g, b_h), flat[0:2], (flat[2:6], flat[6:10]))


def pack_kernel(positions, strengths, radii, pair_list, pair_count, pack, listed, count, sems):
    copies = [
        pltpu.make_async_copy(pair_list, listed, sems.at[0]),
        pltpu.make_async_copy(pair_count, count, sems.at[1]),
        pltpu.make_async_copy(positions, pack.at[0:3], sems.at[2]),
        pltpu.make_async_copy(strengths, pack.at[3:6], sems.at[3]),
        pltpu.make_async_copy(radii, pack.at[6:7], sems.at[4]),
    ]
    for copy in copies:
        copy.start()
    for copy in copies[:2]:
        copy.wait()
    for n, value in enumerate((listed[0, 0, 0, 1], listed[1, 0, 0, 1], count[0, 0])):
        pack[7:8, n * 128 : (n + 1) * 128] = jnp.full((1, 128), value.astype(F32))
    rest = pack.shape[1] - 3 * 128
    pack[7:8, 3 * 128 :] = jnp.zeros((1, rest), F32)
    for copy in copies[2:]:
        copy.wait()


def here(axis):
    return lax.axis_index(axis).astype(jnp.int32)


def stack_kernel(n_pairs, *refs):
    for n in range(n_pairs):
        first, second, both = refs[2 * n], refs[2 * n + 1], refs[n - n_pairs]
        size = first.shape[0]
        both[0:size] = first[...]
        both[size : 2 * size] = second[...]


def place(relative, bits):
    at = 0
    for n in range(bits):
        at += ((relative >> n) & 1) << (bits - 1 - n)
    return at


def listed(pack):
    return [pack[7:8, n * 128 : (n + 1) * 128] for n in range(3)]


def pair_kernel(pack, near_a, far_a, b_0, b_1, b_2, b_3, after, out_a, out_b, apack, bpack, dist, s_col, *rest):
    del after
    sums_a, sums_b, qq, images = rest[0:2], rest[2:4], rest[4:6], rest[6:8]
    k, m, count = [jnp.max(value).astype(jnp.int32) for value in listed(pack)]

    @pl.when(count > 1)
    def _():
        from_a = k ^ here("col")
        from_b = m ^ here("row")
        at = place(from_a >> 1, near_a.shape[0].bit_length() - 1)
        apack[...] = jnp.where(from_a % 2 == 0, near_a[at], far_a[at])
        at = place(from_b >> 2, b_0.shape[0].bit_length() - 1)
        for n, block in enumerate((b_0, b_1, b_2, b_3)):

            @pl.when(from_b % 4 == n)
            def _(block=block):
                bpack[...] = block[at]

        columns(apack[...], dist, s_col)
        right = distances(bpack[...])[1]
        feat_a, feat_b = features(apack[...]), features(bpack[...])
        interact_both(dist, s_col, right, halves(bpack[...]), feat_a, feat_b, qq, images, sums_a, sums_b)
        store_dense(out_a, finish(apack[...], sums_a[0][...], sums_a[1][...]))
        store_dense(out_b, finish(bpack[...], sums_b[0][...], sums_b[1][...]))


def merge_kernel(axis, n_parts, *refs):
    parts, packs, (keep, send) = refs[:n_parts], refs[n_parts:-2], refs[-2:]
    at = here(axis)
    total = onward = jnp.zeros(keep.shape, F32)
    for n, part in enumerate(parts):
        relative = 2 * n
        if axis == "col":
            k, m, count = listed(packs[0][place(n, packs[0].shape[0].bit_length() - 1)])
            target = jnp.where(count > 1, k, -1.0)
        else:
            run = packs[1] if relative & 2 else packs[0]
            k, m, count = listed(run[place(relative >> 2, run.shape[0].bit_length() - 1)])
            itself = (k == here("col").astype(F32)) & (m == (at ^ relative).astype(F32))
            target = jnp.where((count > 1) & ~itself, m, -1.0)
        block = part[...]
        total += jnp.where(target == at.astype(F32), block, 0.0)
        onward += jnp.where(target == (at ^ 1).astype(F32), block, 0.0)
    keep[...] = total
    send[...] = onward


def sum_kernel(keep_a, keep_b, part_a, part_b, *refs):
    own, (velocity, stretching) = refs[:-2], refs[-2:]
    total = load_dense(keep_a[...] + keep_b[...] + part_a[...] + part_b[...], 6)
    total += jnp.concatenate([chunk[...] for chunk in own], axis=1)
    velocity[...] = total[0:3]
    stretching[...] = total[3:6]


def own_work(cols):
    return [
        pltpu.VMEM((G_ROWS, cols), F32),
        pltpu.VMEM((H_ROWS, cols), F32),
        *[pltpu.VMEM((UNIT, UNIT), F32)] * 2,
        *[pltpu.VMEM((UNIT, UNIT), BF16)] * 8,
    ]


def pair_work(g):
    return [
        *[pltpu.VMEM((8, g), F32)] * 2,
        pltpu.VMEM((g, Q_ROWS), BF16),
        pltpu.VMEM((g, 8), F32),
        *[pltpu.VMEM((G_ROWS, g), F32), pltpu.VMEM((H_ROWS, g), F32)] * 2,
        *[pltpu.VMEM((g, UNIT), F32)] * 2,
        *[pltpu.VMEM((g, 4 * UNIT), BF16)] * 2,
    ]


def swap(block, axis, size, step):
    return lax.ppermute(block, axis, [(i, i ^ step) for i in range(size)])


def spread(block, axis, size):
    return [block] + [swap(block, axis, size, s) for s in range(2, size, 2)]


def local(n_row, n_col, positions, strengths, radii, pair_list, pair_count):
    g = radii.shape[0]
    part = g // 4
    hbm_spec = pl.BlockSpec(memory_space=pltpu.HBM)
    vmem_spec = pl.BlockSpec(memory_space=pltpu.VMEM)
    params = pltpu.CompilerParams(vmem_limit_bytes=VMEM)
    block = jax.ShapeDtypeStruct((8, g), F32)
    chunk = jax.ShapeDtypeStruct((6, part), F32)
    dense = jax.ShapeDtypeStruct((6 * g // 128, 128), F32)
    chunk_cost = pl.CostEstimate(flops=30 * g * part, bytes_accessed=64 * g, transcendentals=g * part)
    chunk_call = functools.partial(
        pl.pallas_call, scratch_shapes=own_work(part), compiler_params=params, cost_estimate=chunk_cost
    )

    def later(n, after):
        return chunk_call(
            functools.partial(later_kernel, n),
            out_shape=chunk,
            in_specs=[vmem_spec] * 7,
            out_specs=vmem_spec,
            name=f"own_{n}",
        )(pack, *common, after)

    pack = pl.pallas_call(
        pack_kernel,
        out_shape=block,
        in_specs=[hbm_spec] * 5,
        out_specs=vmem_spec,
        scratch_shapes=[
            pltpu.SMEM(pair_list.shape, jnp.int32),
            pltpu.SMEM(pair_count.shape, jnp.int32),
            pltpu.SemaphoreType.DMA((5,)),
        ],
        name="pack_group",
    )(positions, strengths, radii[None], pair_list, pair_count)

    own = []
    common = ()
    near_a, have_b = pack[None], pack[None]
    after = pack
    for stage in range(n_col.bit_length() - 1):
        step_a, step_b = n_col >> (1 + stage), n_row >> (1 + stage)
        far_a = swap(near_a, "col", n_col, step_a)
        if step_b >= 2:
            far_b = swap(have_b, "row", n_row, step_b)
            if step_b == 2:
                next_b = swap(have_b, "row", n_row, 1)
        elif step_b == 1:
            last_b = swap(far_b, "row", n_row, 1)
        if stage == 0:
            chunk_0, *common = chunk_call(
                first_kernel,
                out_shape=(
                    chunk,
                    jax.ShapeDtypeStruct((g, Q_ROWS), BF16),
                    jax.ShapeDtypeStruct((g, 8), F32),
                    jax.ShapeDtypeStruct((Q_ROWS, g), BF16),
                    jax.ShapeDtypeStruct((G_ROWS, g), BF16),
                    jax.ShapeDtypeStruct((H_ROWS, g), BF16),
                ),
                in_specs=[vmem_spec],
                out_specs=(vmem_spec,) * 6,
                name="own_first",
            )(pack)
            own.append(chunk_0)
        elif stage < 3:
            own.append(later(stage, after))
        if step_a == 1:
            break
        runs = [(near_a, far_a)]
        if step_b > 2:
            runs.append((have_b, far_b))
        arrived = [own[-1], last_b if step_b == 1 else far_b]
        if step_b == 2:
            arrived.append(next_b)
        stacked = pl.pallas_call(
            functools.partial(stack_kernel, len(runs)),
            out_shape=tuple(jax.ShapeDtypeStruct((2 * n.shape[0], 8, g), F32) for n, _ in runs),
            in_specs=[vmem_spec] * (2 * len(runs) + len(arrived)),
            out_specs=(vmem_spec,) * len(runs),
            compiler_params=params,
            name="stack_groups",
        )(*[block for run in runs for block in run], *arrived)
        near_a = after = stacked[0]
        if len(runs) > 1:
            have_b = stacked[1]

    side_a, side_b = pl.pallas_call(
        pair_kernel,
        out_shape=(dense, dense),
        in_specs=[vmem_spec] * 8,
        out_specs=(vmem_spec, vmem_spec),
        scratch_shapes=pair_work(g),
        compiler_params=params,
        cost_estimate=pl.CostEstimate(flops=60 * g * g, bytes_accessed=128 * g, transcendentals=g * g),
        name="listed_pair",
    )(pack, near_a, far_a, have_b, next_b, far_b, last_b, own[-1])

    def merge(parts, packs, axis):
        return pl.pallas_call(
            functools.partial(merge_kernel, axis, len(parts)),
            out_shape=(dense,) * 2,
            in_specs=[vmem_spec] * (len(parts) + len(packs)),
            out_specs=(vmem_spec,) * 2,
            compiler_params=params,
            name="merge_" + axis,
        )(*parts, *packs)

    parts_a = spread(side_a, "col", n_col)
    parts_b = spread(side_b, "row", n_row)
    keep_b, send_b = merge(parts_b, [have_b, far_b], "row")
    far_b = swap(send_b, "row", n_row, 1)
    keep_a, send_a = merge(parts_a, [near_a], "col")
    far_a = swap(send_a, "col", n_col, 1)
    own.append(later(3, keep_a))

    three = jax.ShapeDtypeStruct((3, g), F32)
    return pl.pallas_call(
        sum_kernel,
        out_shape=(three, three),
        in_specs=[vmem_spec] * 8,
        out_specs=(vmem_spec, vmem_spec),
        compiler_params=params,
        name="sum_parts",
    )(keep_a, keep_b, far_a, far_b, *own)


def solution(mesh):
    placed = (
        P(None, ("row", "col")),
        P(None, ("row", "col")),
        P(("row", "col")),
        P(None, "row", "col", None),
        P("row", "col"),
    )
    return jax.shard_map(
        functools.partial(local, mesh.shape["row"], mesh.shape["col"]),
        mesh=mesh,
        in_specs=placed,
        out_specs=(P(None, ("row", "col")), P(None, ("row", "col"))),
        check_vma=False,
    )
```

```python
import functools
import math

import jax
import jax.numpy as jnp
from jax import lax
from jax.experimental import pallas as pl
from jax.experimental.pallas import tpu as pltpu
from jax.sharding import PartitionSpec as P

F32 = jnp.float32
BF16 = jnp.bfloat16
UNIT = 256
STRIP = 16
G_ROWS = 32
H_ROWS = 96
Q_ROWS = 32
G_SCALE = -1.5 / (4.0 * math.pi)
H_SCALE = 7.5 / (4.0 * math.pi)
VMEM = 48 * 1024 * 1024


def cross(u, v):
    return jnp.concatenate(
        [
            u[1:2] * v[2:3] - u[2:3] * v[1:2],
            u[2:3] * v[0:1] - u[0:1] * v[2:3],
            u[0:1] * v[1:2] - u[1:2] * v[0:1],
        ]
    )


def split(f):
    hi = f.astype(BF16).astype(F32)
    mid = (f - hi).astype(BF16).astype(F32)
    return [hi, mid, (f - hi) - mid]


def features(pack):
    pos = pack[0:3] - 0.5
    st = pack[3:6]
    e0 = jnp.concatenate([st, cross(pos, st), jnp.zeros((2, pack.shape[1]), F32)])
    moments = jnp.concatenate([e0, pos[0:1] * e0, pos[1:2] * e0, pos[2:3] * e0])
    for_g = jnp.concatenate(split(e0) + [jnp.zeros_like(e0)]).astype(BF16)
    return for_g, jnp.concatenate(split(moments)).astype(BF16)


def finish(pack, g, h):
    g = g[0:8] + g[8:16] + g[16:24]
    h = h[0:32] + h[32:64] + h[64:96]
    pos = pack[0:3] - 0.5
    st = pack[3:6]
    dot = jnp.sum(pos * st, axis=0, keepdims=True)
    d = dot * h[0:8] - st[0:1] * h[8:16] - st[1:2] * h[16:24] - st[2:3] * h[24:32]
    vel = G_SCALE * (cross(pos, g[0:3]) - g[3:6])
    stretch = G_SCALE * cross(st, g[0:3]) + H_SCALE * (cross(pos, d[0:3]) - d[3:6])
    return jnp.concatenate([vel, stretch])


def store_dense(out, value):
    rows = value.shape[0]
    for n in range(value.shape[1] // 128):
        out[n * rows : (n + 1) * rows, :] = value[:, n * 128 : (n + 1) * 128]


def load_dense(value, rows):
    return jnp.concatenate([value[n : n + rows] for n in range(0, value.shape[0], rows)], axis=1)


def strip(qq, s, images, r):
    ghi, glo, hhi, hlo = images
    here = slice(r, r + STRIP)
    t = lax.rsqrt(qq)
    t2 = t * t
    v = s * t2
    t3 = t2 * t
    g = t3 * (v + 2.0 / 3.0)
    h = (t3 * t2) * (v + 0.4)
    high = g.astype(BF16)
    ghi[here] = high
    glo[here] = (g - high.astype(F32)).astype(BF16)
    high = h.astype(BF16)
    hhi[here] = high
    hlo[here] = (h - high.astype(F32)).astype(BF16)


def down(f, image):
    return jnp.dot(f, image, preferred_element_type=F32)


def across(f, image):
    return lax.dot_general(f, image, (((1,), (1,)), ((), ())), preferred_element_type=F32)


def halves(pack):
    return 0.5 * pack[6:7] * pack[6:7]


def distances(pack):
    pos = pack[0:3] - 0.5
    x1, x2, x3 = split(pos)
    norm = jnp.concatenate(split(jnp.sum(pos * pos, axis=0, keepdims=True) + halves(pack)))
    one = jnp.ones_like(norm)
    blank = jnp.zeros((8, pack.shape[1]), F32)
    left = [-2.0 * x for x in (x1, x1, x2, x2, x1, x3)] + [norm, one, blank]
    right = [x1, x2, x1, x2, x3, x1, one, norm, blank]
    return jnp.concatenate(left), jnp.concatenate(right).astype(BF16)


def columns(pack, dist, s_col):
    left, right = distances(pack)
    blank = jnp.zeros((7, pack.shape[1]), F32)
    turned = jnp.transpose(jnp.concatenate([left[:24], halves(pack), blank]))
    s_col[...] = turned
    dist[...] = turned.astype(BF16)
    return right


def interact(dist_a, s_a, dist_b, s_b, feat_a, qq, slots, sums_b):
    for total in sums_b:
        total[...] = jnp.zeros_like(total)

    def products(i, j, images):
        pi, pj = slice(i, i + UNIT), slice(j, j + UNIT)
        steps = []

        def add(total, f, high, low):
            total[:, pj] += down(f, high[...]) + down(f, low[...])

        for kind in range(2):
            f = feat_a[kind][:, pi]
            steps.append(functools.partial(add, sums_b[kind], f, *images[2 * kind : 2 * kind + 2]))
        return steps

    def measure(unit, into):
        i, j = unit
        into[...] = down(dist_a[i : i + UNIT, :], dist_b[:, j : j + UNIT])

    n_strip = UNIT // STRIP
    units = [(i, j) for j in range(0, s_b.shape[1], UNIT) for i in range(0, s_a.shape[0], UNIT)]
    measure(units[0], qq[0])
    waiting = []
    for count, (i, j) in enumerate(units):
        images = slots[count % 2]
        if count + 1 < len(units):
            waiting.insert(0, functools.partial(measure, units[count + 1], qq[(count + 1) % 2]))
        per = n_strip // max(1, len(waiting))
        row = jnp.broadcast_to(s_b[0:1, j : j + UNIT], (STRIP, UNIT))
        for n in range(n_strip):
            at = slice(i + n * STRIP, i + (n + 1) * STRIP)
            here = slice(n * STRIP, (n + 1) * STRIP)
            strip(qq[count % 2][here, :], s_a[at, 24:25] + row, images, n * STRIP)
            if waiting and (n + 1) % per == 0:
                waiting.pop(0)()
        for step in waiting:
            step()
        waiting = products(i, j, images)
    for step in waiting:
        step()


def interact_both(dist_a, s_a, dist_b, s_b, feat_a, feat_b, qq, images, sums_a, sums_b):
    rows, n = s_a.shape[0], UNIT
    blocks, chunks = s_b.shape[1] // n, rows // n
    half = rows // 2

    def measure(block, c):
        here, part = slice(c * n, (c + 1) * n), slice(block * n, (block + 1) * n)
        qq[block % 2][here, :] = down(dist_a[here, :], dist_b[:, part])

    def onto_a(block, c, kind):
        here, part = slice(c * n, (c + 1) * n), slice(block * n, (block + 1) * n)
        f = jnp.concatenate([feat_b[kind][:, part]] * 2, axis=1)
        share = across(f, images[block % 2][here, 2 * kind * n : 2 * (kind + 1) * n])
        sums_a[kind][:, here] = share if block == 0 else sums_a[kind][:, here] + share

    def onto_b(block, later, kind):
        here, part = slice(later * half, (later + 1) * half), slice(block * n, (block + 1) * n)
        image = images[block % 2]
        at = 2 * kind * n
        f = feat_a[kind][:, here]
        share = down(f, image[here, at : at + n]) + down(f, image[here, at + n : at + 2 * n])
        sums_b[kind][:, part] = sums_b[kind][:, part] + share if later else share

    for c in range(chunks):
        measure(0, c)
    ready, delayed = [], []
    for block in range(blocks):
        image = images[block % 2]
        part = slice(block * n, (block + 1) * n)
        slots = [image.at[:, m * n : (m + 1) * n] for m in range(4)]
        row = jnp.broadcast_to(s_b[0:1, part], (STRIP, n))
        for c in range(chunks):
            todo, ready, delayed = ready, delayed, []
            if block + 1 < blocks:
                todo.append(functools.partial(measure, block + 1, c))
            n_strip = n // STRIP
            per = max(1, n_strip // max(1, len(todo)))
            for m in range(n_strip):
                here = slice(c * n + m * STRIP, c * n + (m + 1) * STRIP)
                strip(qq[block % 2][here, :], s_a[here, 24:25] + row, slots, c * n + m * STRIP)
                if todo and (m + 1) % per == 0:
                    todo.pop(0)()
            for step in todo:
                step()
            for kind in range(2):
                ready.append(functools.partial(onto_a, block, c, kind))
            if (c + 1) % (chunks // 2) == 0:
                later = (c + 1) // (chunks // 2) - 1
                ready.append(functools.partial(onto_b, block, later, 0))
                delayed.append(functools.partial(onto_b, block, later, 1))
    for step in ready + delayed:
        step()


def own_chunk(n, pack, dist, s_col, right, feat, out, sums, qq, slots):
    part = slice(n * out.shape[1], (n + 1) * out.shape[1])
    interact(dist, s_col, right[:, part], halves(pack[:, part]), feat, qq, slots, sums)
    out[...] = finish(pack[:, part], sums[0][...], sums[1][...])


def first_kernel(pack, out, dist, s_col, right, feat_g, feat_h, b_g, b_h, *flat):
    right[...] = columns(pack[...], dist, s_col)
    feat_g[...], feat_h[...] = features(pack[...])
    own_chunk(0, pack, dist, s_col, right, (feat_g, feat_h), out, (b_g, b_h), flat[0:2], (flat[2:6], flat[6:10]))


def later_kernel(n, pack, dist, s_col, right, feat_g, feat_h, after, out, b_g, b_h, *flat):
    del after
    own_chunk(n, pack, dist, s_col, right, (feat_g, feat_h), out, (b_g, b_h), flat[0:2], (flat[2:6], flat[6:10]))


def pack_kernel(positions, strengths, radii, pair_list, pair_count, pack, listed, count, sems):
    copies = [
        pltpu.make_async_copy(pair_list, listed, sems.at[0]),
        pltpu.make_async_copy(pair_count, count, sems.at[1]),
        pltpu.make_async_copy(positions, pack.at[0:3], sems.at[2]),
        pltpu.make_async_copy(strengths, pack.at[3:6], sems.at[3]),
        pltpu.make_async_copy(radii, pack.at[6:7], sems.at[4]),
    ]
    for copy in copies:
        copy.start()
    for copy in copies[:2]:
        copy.wait()
    for n, value in enumerate((listed[0, 0, 0, 1], listed[1, 0, 0, 1], count[0, 0])):
        pack[7:8, n * 128 : (n + 1) * 128] = jnp.full((1, 128), value.astype(F32))
    rest = pack.shape[1] - 3 * 128
    pack[7:8, 3 * 128 :] = jnp.zeros((1, rest), F32)
    for copy in copies[2:]:
        copy.wait()


def here(axis):
    return lax.axis_index(axis).astype(jnp.int32)


def stack_kernel(n_pairs, n_arrived, *refs):
    del n_arrived
    for n in range(n_pairs):
        first, second, both = refs[2 * n], refs[2 * n + 1], refs[n - n_pairs]
        size = first.shape[0]
        both[0:size] = first[...]
        both[size : 2 * size] = second[...]


def place(relative, bits):
    at = 0
    for n in range(bits):
        at += ((relative >> n) & 1) << (bits - 1 - n)
    return at


def listed(pack):
    return [pack[7:8, n * 128 : (n + 1) * 128] for n in range(3)]


def choose(relative, near, far):
    at = place(relative >> 1, near.shape[0].bit_length() - 1)
    return jnp.where(relative % 2 == 0, near[at], far[at])


def prepare_kernel(pack, near, far, after, chosen, right, feat_g, feat_h):
    del after
    m = jnp.max(listed(pack)[1]).astype(jnp.int32)
    chosen[...] = choose(m ^ here("row"), near, far)
    right[...] = distances(chosen[...])[1]
    feat_g[...], feat_h[...] = features(chosen[...])


def pair_kernel(pack, near, far, bpack, right, feat_g, feat_h, after, out_a, out_b, apack, dist, s_col, *rest):
    del after
    sums_a, sums_b, qq, images = rest[0:2], rest[2:4], rest[4:6], rest[6:8]
    k, _, count = [jnp.max(value).astype(jnp.int32) for value in listed(pack)]

    @pl.when(count > 1)
    def _():
        apack[...] = choose(k ^ here("col"), near, far)
        columns(apack[...], dist, s_col)
        feat_a = features(apack[...])
        interact_both(
            dist, s_col, right, halves(bpack[...]), feat_a, (feat_g, feat_h), qq, images, sums_a, sums_b
        )
        store_dense(out_a, finish(apack[...], sums_a[0][...], sums_a[1][...]))
        store_dense(out_b, finish(bpack[...], sums_b[0][...], sums_b[1][...]))


def merge_kernel(axis, n_parts, *refs):
    parts, (near, keep, send) = refs[:n_parts], refs[n_parts:]
    at = here(axis)
    total = onward = jnp.zeros(keep.shape, F32)
    for n, part in enumerate(parts):
        relative = 2 * (n_parts - 1 - n)
        k, m, count = listed(near[place(relative >> 1, near.shape[0].bit_length() - 1)])
        if axis == "col":
            target = jnp.where(count > 1, k, -1.0)
        else:
            itself = (k == here("col").astype(F32)) & (m == (at ^ relative).astype(F32))
            target = jnp.where((count > 1) & ~itself, m, -1.0)
        block = part[...]
        total += jnp.where(target == at.astype(F32), block, 0.0)
        onward += jnp.where(target == (at ^ 1).astype(F32), block, 0.0)
    keep[...] = total
    send[...] = onward


def sum_kernel(keep_a, keep_b, part_a, part_b, *refs):
    own, (velocity, stretching) = refs[:-2], refs[-2:]
    total = load_dense(keep_a[...] + keep_b[...] + part_a[...] + part_b[...], 6)
    total += jnp.concatenate([chunk[...] for chunk in own], axis=1)
    velocity[...] = total[0:3]
    stretching[...] = total[3:6]


def own_work(cols):
    return [
        pltpu.VMEM((G_ROWS, cols), F32),
        pltpu.VMEM((H_ROWS, cols), F32),
        *[pltpu.VMEM((UNIT, UNIT), F32)] * 2,
        *[pltpu.VMEM((UNIT, UNIT), BF16)] * 8,
    ]


def pair_work(g):
    return [
        pltpu.VMEM((8, g), F32),
        pltpu.VMEM((g, Q_ROWS), BF16),
        pltpu.VMEM((g, Q_ROWS), F32),
        *[pltpu.VMEM((G_ROWS, g), F32), pltpu.VMEM((H_ROWS, g), F32)] * 2,
        *[pltpu.VMEM((g, UNIT), F32)] * 2,
        *[pltpu.VMEM((g, 4 * UNIT), BF16)] * 2,
    ]


def swap(block, axis, size, step):
    return lax.ppermute(block, axis, [(i, i ^ step) for i in range(size)])


def spread(block, axis, size):
    return [swap(block, axis, size, s) for s in range(size - 2, 0, -2)] + [block]


def local(n_row, n_col, positions, strengths, radii, pair_list, pair_count):
    g = radii.shape[0]
    part = g // 4
    hbm_spec = pl.BlockSpec(memory_space=pltpu.HBM)
    vmem_spec = pl.BlockSpec(memory_space=pltpu.VMEM)
    params = pltpu.CompilerParams(vmem_limit_bytes=VMEM)
    block = jax.ShapeDtypeStruct((8, g), F32)
    chunk = jax.ShapeDtypeStruct((6, part), F32)
    dense = jax.ShapeDtypeStruct((6 * g // 128, 128), F32)
    chunk_cost = pl.CostEstimate(flops=30 * g * part, bytes_accessed=64 * g, transcendentals=g * part)
    chunk_call = functools.partial(
        pl.pallas_call, scratch_shapes=own_work(part), compiler_params=params, cost_estimate=chunk_cost
    )

    def later(n, after):
        return chunk_call(
            functools.partial(later_kernel, n),
            out_shape=chunk,
            in_specs=[vmem_spec] * 7,
            out_specs=vmem_spec,
            name=f"own_{n}",
        )(pack, *common, after)

    pack = pl.pallas_call(
        pack_kernel,
        out_shape=block,
        in_specs=[hbm_spec] * 5,
        out_specs=vmem_spec,
        scratch_shapes=[
            pltpu.SMEM(pair_list.shape, jnp.int32),
            pltpu.SMEM(pair_count.shape, jnp.int32),
            pltpu.SemaphoreType.DMA((5,)),
        ],
        name="pack_group",
    )(positions, strengths, radii[None], pair_list, pair_count)

    own = []
    near_a, near_b = pack[None], pack[None]
    for stage in range(n_col.bit_length() - 1):
        step_a, step_b = n_col >> (1 + stage), n_row >> (1 + stage)
        far_a = swap(near_a, "col", n_col, step_a)
        if step_b:
            far_b = swap(near_b, "row", n_row, step_b)
        if step_a == 1:
            break
        if stage == 0:
            chunk_0, *common = chunk_call(
                first_kernel,
                out_shape=(
                    chunk,
                    jax.ShapeDtypeStruct((g, Q_ROWS), BF16),
                    jax.ShapeDtypeStruct((g, Q_ROWS), F32),
                    jax.ShapeDtypeStruct((Q_ROWS, g), BF16),
                    jax.ShapeDtypeStruct((G_ROWS, g), BF16),
                    jax.ShapeDtypeStruct((H_ROWS, g), BF16),
                ),
                in_specs=[vmem_spec],
                out_specs=(vmem_spec,) * 6,
                name="own_first",
            )(pack)
            own.append(chunk_0)
        elif stage == 1:
            own.append(later(1, near_a))
            own.append(later(2, near_a))
        arrived = own[-2:] + [far_b]
        runs = [(near_a, far_a)]
        if step_b > 1:
            runs.append((near_b, far_b))
        stacked = pl.pallas_call(
            functools.partial(stack_kernel, len(runs), len(arrived)),
            out_shape=tuple(jax.ShapeDtypeStruct((2 * n.shape[0], 8, g), F32) for n, _ in runs),
            in_specs=[vmem_spec] * (2 * len(runs) + len(arrived)),
            out_specs=(vmem_spec,) * len(runs),
            compiler_params=params,
            name="stack_groups",
        )(*[block for run in runs for block in run], *arrived)
        near_a = stacked[0]
        if len(runs) > 1:
            near_b = stacked[1]

    prepared = pl.pallas_call(
        prepare_kernel,
        out_shape=(
            block,
            jax.ShapeDtypeStruct((Q_ROWS, g), BF16),
            jax.ShapeDtypeStruct((G_ROWS, g), BF16),
            jax.ShapeDtypeStruct((H_ROWS, g), BF16),
        ),
        in_specs=[vmem_spec] * 4,
        out_specs=(vmem_spec,) * 4,
        compiler_params=params,
        cost_estimate=pl.CostEstimate(flops=g * g, bytes_accessed=64 * g, transcendentals=0),
        name="prepare_group",
    )(pack, near_b, far_b, near_a)

    side_a, side_b = pl.pallas_call(
        pair_kernel,
        out_shape=(dense, dense),
        in_specs=[vmem_spec] * 8,
        out_specs=(vmem_spec, vmem_spec),
        scratch_shapes=pair_work(g),
        compiler_params=params,
        cost_estimate=pl.CostEstimate(flops=60 * g * g, bytes_accessed=128 * g, transcendentals=g * g),
        name="listed_pair",
    )(pack, near_a, far_a, *prepared, own[-1])

    def merge(parts, near, axis):
        return pl.pallas_call(
            functools.partial(merge_kernel, axis, len(parts)),
            out_shape=(dense,) * 2,
            in_specs=[vmem_spec] * (len(parts) + 1),
            out_specs=(vmem_spec,) * 2,
            compiler_params=params,
            name="merge_" + axis,
        )(*parts, near)

    parts_a = spread(side_a, "col", n_col)
    parts_b = spread(side_b, "row", n_row)
    keep_b, send_b = merge(parts_b, near_b, "row")
    far_b = swap(send_b, "row", n_row, 1)
    keep_a, send_a = merge(parts_a, near_a, "col")
    far_a = swap(send_a, "col", n_col, 1)
    own.append(later(3, keep_a))

    three = jax.ShapeDtypeStruct((3, g), F32)
    return pl.pallas_call(
        sum_kernel,
        out_shape=(three, three),
        in_specs=[vmem_spec] * 8,
        out_specs=(vmem_spec, vmem_spec),
        compiler_params=params,
        name="sum_parts",
    )(keep_a, keep_b, far_a, far_b, *own)


def solution(mesh):
    placed = (
        P(None, ("row", "col")),
        P(None, ("row", "col")),
        P(("row", "col")),
        P(None, "row", "col", None),
        P("row", "col"),
    )
    return jax.shard_map(
        functools.partial(local, mesh.shape["row"], mesh.shape["col"]),
        mesh=mesh,
        in_specs=placed,
        out_specs=(P(None, ("row", "col")), P(None, ("row", "col"))),
        check_vma=False,
    )
```

```python
import functools
import math

import jax
import jax.numpy as jnp
from jax import lax
from jax.experimental import pallas as pl
from jax.experimental.pallas import tpu as pltpu
from jax.sharding import PartitionSpec as P

F32 = jnp.float32
BF16 = jnp.bfloat16
UNIT = 256
STRIP = 16
G_ROWS = 32
H_ROWS = 96
Q_ROWS = 32
G_SCALE = -1.5 / (4.0 * math.pi)
H_SCALE = 7.5 / (4.0 * math.pi)
VMEM = 48 * 1024 * 1024


def cross(u, v):
    return jnp.concatenate(
        [
            u[1:2] * v[2:3] - u[2:3] * v[1:2],
            u[2:3] * v[0:1] - u[0:1] * v[2:3],
            u[0:1] * v[1:2] - u[1:2] * v[0:1],
        ]
    )


def split(f):
    hi = f.astype(BF16).astype(F32)
    mid = (f - hi).astype(BF16).astype(F32)
    return [hi, mid, (f - hi) - mid]


def features(pack):
    pos = pack[0:3] - 0.5
    st = pack[3:6]
    e0 = jnp.concatenate([st, cross(pos, st), jnp.zeros((2, pack.shape[1]), F32)])
    moments = jnp.concatenate([e0, pos[0:1] * e0, pos[1:2] * e0, pos[2:3] * e0])
    for_g = jnp.concatenate(split(e0) + [jnp.zeros_like(e0)]).astype(BF16)
    return for_g, jnp.concatenate(split(moments)).astype(BF16)


def finish(pack, g, h):
    g = g[0:8] + g[8:16] + g[16:24]
    h = h[0:32] + h[32:64] + h[64:96]
    pos = pack[0:3] - 0.5
    st = pack[3:6]
    dot = jnp.sum(pos * st, axis=0, keepdims=True)
    d = dot * h[0:8] - st[0:1] * h[8:16] - st[1:2] * h[16:24] - st[2:3] * h[24:32]
    vel = G_SCALE * (cross(pos, g[0:3]) - g[3:6])
    stretch = G_SCALE * cross(st, g[0:3]) + H_SCALE * (cross(pos, d[0:3]) - d[3:6])
    return jnp.concatenate([vel, stretch])


def store_dense(out, value):
    rows = value.shape[0]
    for n in range(value.shape[1] // 128):
        out[n * rows : (n + 1) * rows, :] = value[:, n * 128 : (n + 1) * 128]


def load_dense(value, rows):
    return jnp.concatenate([value[n : n + rows] for n in range(0, value.shape[0], rows)], axis=1)


def strip(qq, s, images, r):
    ghi, glo, hhi, hlo = images
    here = slice(r, r + STRIP)
    t = lax.rsqrt(qq)
    t2 = t * t
    v = s * t2
    t3 = t2 * t
    g = t3 * (v + 2.0 / 3.0)
    h = (t3 * t2) * (v + 0.4)
    high = g.astype(BF16)
    ghi[here] = high
    glo[here] = (g - high.astype(F32)).astype(BF16)
    high = h.astype(BF16)
    hhi[here] = high
    hlo[here] = (h - high.astype(F32)).astype(BF16)


def down(f, image):
    return jnp.dot(f, image, preferred_element_type=F32)


def across(f, image):
    return lax.dot_general(f, image, (((1,), (1,)), ((), ())), preferred_element_type=F32)


def halves(pack):
    return 0.5 * pack[6:7] * pack[6:7]


def distances(pack):
    pos = pack[0:3] - 0.5
    x1, x2, x3 = split(pos)
    norm = jnp.concatenate(split(jnp.sum(pos * pos, axis=0, keepdims=True) + halves(pack)))
    one = jnp.ones_like(norm)
    blank = jnp.zeros((8, pack.shape[1]), F32)
    left = [-2.0 * x for x in (x1, x1, x2, x2, x1, x3)] + [norm, one, blank]
    right = [x1, x2, x1, x2, x3, x1, one, norm, blank]
    return jnp.concatenate(left), jnp.concatenate(right).astype(BF16)


def columns(pack, dist, s_col):
    left, right = distances(pack)
    blank = jnp.zeros((7, pack.shape[1]), F32)
    turned = jnp.transpose(jnp.concatenate([left[:24], halves(pack), blank]))
    s_col[...] = turned
    dist[...] = turned.astype(BF16)
    return right


def outline(pack, factor):
    pos = pack[0:3] - 0.5
    half = halves(pack)
    norm = jnp.sum(pos * pos, axis=0, keepdims=True) + half
    return jnp.concatenate([factor * pos, norm, half, jnp.zeros((3, pack.shape[1]), F32)])


def interact(dist_a, s_a, dist_b, s_b, feat_a, qq, slots, sums_b):
    for total in sums_b:
        total[...] = jnp.zeros_like(total)

    def products(i, j, images):
        pi, pj = slice(i, i + UNIT), slice(j, j + UNIT)
        steps = []

        def add(total, f, high, low):
            total[:, pj] += down(f, high[...]) + down(f, low[...])

        for kind in range(2):
            f = feat_a[kind][:, pi]
            steps.append(functools.partial(add, sums_b[kind], f, *images[2 * kind : 2 * kind + 2]))
        return steps

    def measure(unit, into):
        i, j = unit
        into[...] = down(dist_a[i : i + UNIT, :], dist_b[:, j : j + UNIT])

    n_strip = UNIT // STRIP
    units = [(i, j) for j in range(0, s_b.shape[1], UNIT) for i in range(0, s_a.shape[0], UNIT)]
    measure(units[0], qq[0])
    waiting = []
    for count, (i, j) in enumerate(units):
        images = slots[count % 2]
        if count + 1 < len(units):
            waiting.insert(0, functools.partial(measure, units[count + 1], qq[(count + 1) % 2]))
        per = n_strip // max(1, len(waiting))
        row = jnp.broadcast_to(s_b[0:1, j : j + UNIT], (STRIP, UNIT))
        for n in range(n_strip):
            at = slice(i + n * STRIP, i + (n + 1) * STRIP)
            here = slice(n * STRIP, (n + 1) * STRIP)
            strip(qq[count % 2][here, :], s_a[at, 24:25] + row, images, n * STRIP)
            if waiting and (n + 1) % per == 0:
                waiting.pop(0)()
        for step in waiting:
            step()
        waiting = products(i, j, images)
    for step in waiting:
        step()


def interact_both(col, rows_b, feat_a, feat_b, images, sums_a, sums_b):
    rows, n = col.shape[0], UNIT
    blocks, chunks = rows_b.shape[1] // n, rows // n
    half = rows // 2

    def onto_a(block, c, kind):
        here, part = slice(c * n, (c + 1) * n), slice(block * n, (block + 1) * n)
        f = jnp.concatenate([feat_b[kind][:, part]] * 2, axis=1)
        share = across(f, images[block % 2][here, 2 * kind * n : 2 * (kind + 1) * n])
        sums_a[kind][:, here] = share if block == 0 else sums_a[kind][:, here] + share

    def onto_b(block, later, kind):
        here, part = slice(later * half, (later + 1) * half), slice(block * n, (block + 1) * n)
        image = images[block % 2]
        at = 2 * kind * n
        f = feat_a[kind][:, here]
        share = down(f, image[here, at : at + n]) + down(f, image[here, at + n : at + 2 * n])
        sums_b[kind][:, part] = sums_b[kind][:, part] + share if later else share

    ready, delayed = [], []
    for block in range(blocks):
        image = images[block % 2]
        part = slice(block * n, (block + 1) * n)
        slots = [image.at[:, m * n : (m + 1) * n] for m in range(4)]
        row = [jnp.broadcast_to(rows_b[m : m + 1, part], (STRIP, n)) for m in range(5)]
        for c in range(chunks):
            todo, ready, delayed = ready, delayed, []
            n_strip = n // STRIP
            per = max(1, n_strip // max(1, len(todo)))
            for m in range(n_strip):
                here = slice(c * n + m * STRIP, c * n + (m + 1) * STRIP)
                own = [col[here, q : q + 1] for q in range(5)]
                qq = own[0] * row[0] + own[1] * row[1] + own[2] * row[2] + (own[3] + row[3])
                strip(qq, own[4] + row[4], slots, c * n + m * STRIP)
                if todo and (m + 1) % per == 0:
                    todo.pop(0)()
            for step in todo:
                step()
            for kind in range(2):
                ready.append(functools.partial(onto_a, block, c, kind))
            if (c + 1) % (chunks // 2) == 0:
                later = (c + 1) // (chunks // 2) - 1
                ready.append(functools.partial(onto_b, block, later, 0))
                delayed.append(functools.partial(onto_b, block, later, 1))
    for step in ready + delayed:
        step()


def own_chunk(n, pack, dist, s_col, right, feat, out, sums, qq, slots):
    part = slice(n * out.shape[1], (n + 1) * out.shape[1])
    interact(dist, s_col, right[:, part], halves(pack[:, part]), feat, qq, slots, sums)
    out[...] = finish(pack[:, part], sums[0][...], sums[1][...])


def first_kernel(pack, out, dist, s_col, right, feat_g, feat_h, b_g, b_h, *flat):
    right[...] = columns(pack[...], dist, s_col)
    feat_g[...], feat_h[...] = features(pack[...])
    own_chunk(0, pack, dist, s_col, right, (feat_g, feat_h), out, (b_g, b_h), flat[0:2], (flat[2:6], flat[6:10]))


def later_kernel(n, pack, dist, s_col, right, feat_g, feat_h, after, out, b_g, b_h, *flat):
    del after
    own_chunk(n, pack, dist, s_col, right, (feat_g, feat_h), out, (b_g, b_h), flat[0:2], (flat[2:6], flat[6:10]))


def pack_kernel(positions, strengths, radii, pair_list, pair_count, pack, listed, count, sems):
    copies = [
        pltpu.make_async_copy(pair_list, listed, sems.at[0]),
        pltpu.make_async_copy(pair_count, count, sems.at[1]),
        pltpu.make_async_copy(positions, pack.at[0:3], sems.at[2]),
        pltpu.make_async_copy(strengths, pack.at[3:6], sems.at[3]),
        pltpu.make_async_copy(radii, pack.at[6:7], sems.at[4]),
    ]
    for copy in copies:
        copy.start()
    for copy in copies[:2]:
        copy.wait()
    for n, value in enumerate((listed[0, 0, 0, 1], listed[1, 0, 0, 1], count[0, 0])):
        pack[7:8, n * 128 : (n + 1) * 128] = jnp.full((1, 128), value.astype(F32))
    rest = pack.shape[1] - 3 * 128
    pack[7:8, 3 * 128 :] = jnp.zeros((1, rest), F32)
    for copy in copies[2:]:
        copy.wait()


def here(axis):
    return lax.axis_index(axis).astype(jnp.int32)


def stack_kernel(n_pairs, n_arrived, *refs):
    del n_arrived
    for n in range(n_pairs):
        first, second, both = refs[2 * n], refs[2 * n + 1], refs[n - n_pairs]
        size = first.shape[0]
        both[0:size] = first[...]
        both[size : 2 * size] = second[...]


def place(relative, bits):
    at = 0
    for n in range(bits):
        at += ((relative >> n) & 1) << (bits - 1 - n)
    return at


def listed(pack):
    return [pack[7:8, n * 128 : (n + 1) * 128] for n in range(3)]


def choose(relative, near, far):
    at = place(relative >> 1, near.shape[0].bit_length() - 1)
    return jnp.where(relative % 2 == 0, near[at], far[at])


def prepare_kernel(pack, near, far, after, chosen, rows, feat_g, feat_h):
    del after
    m = jnp.max(listed(pack)[1]).astype(jnp.int32)
    chosen[...] = choose(m ^ here("row"), near, far)
    rows[...] = outline(chosen[...], 1.0)
    feat_g[...], feat_h[...] = features(chosen[...])


def pair_kernel(pack, near, far, bpack, rows_b, feat_g, feat_h, after, out_a, out_b, apack, col, *rest):
    del after
    sums_a, sums_b, images = rest[0:2], rest[2:4], rest[4:6]
    k, _, count = [jnp.max(value).astype(jnp.int32) for value in listed(pack)]

    @pl.when(count > 1)
    def _():
        apack[...] = choose(k ^ here("col"), near, far)
        col[...] = jnp.transpose(outline(apack[...], -2.0))
        interact_both(col, rows_b, features(apack[...]), (feat_g, feat_h), images, sums_a, sums_b)
        store_dense(out_a, finish(apack[...], sums_a[0][...], sums_a[1][...]))
        store_dense(out_b, finish(bpack[...], sums_b[0][...], sums_b[1][...]))


def merge_kernel(axis, n_parts, *refs):
    parts, (near, keep, send) = refs[:n_parts], refs[n_parts:]
    at = here(axis)
    total = onward = jnp.zeros(keep.shape, F32)
    for n, part in enumerate(parts):
        relative = 2 * (n_parts - 1 - n)
        k, m, count = listed(near[place(relative >> 1, near.shape[0].bit_length() - 1)])
        if axis == "col":
            target = jnp.where(count > 1, k, -1.0)
        else:
            itself = (k == here("col").astype(F32)) & (m == (at ^ relative).astype(F32))
            target = jnp.where((count > 1) & ~itself, m, -1.0)
        block = part[...]
        total += jnp.where(target == at.astype(F32), block, 0.0)
        onward += jnp.where(target == (at ^ 1).astype(F32), block, 0.0)
    keep[...] = total
    send[...] = onward


def sum_kernel(keep_a, keep_b, part_a, part_b, *refs):
    own, (velocity, stretching) = refs[:-2], refs[-2:]
    total = load_dense(keep_a[...] + keep_b[...] + part_a[...] + part_b[...], 6)
    total += jnp.concatenate([chunk[...] for chunk in own], axis=1)
    velocity[...] = total[0:3]
    stretching[...] = total[3:6]


def own_work(cols):
    return [
        pltpu.VMEM((G_ROWS, cols), F32),
        pltpu.VMEM((H_ROWS, cols), F32),
        *[pltpu.VMEM((UNIT, UNIT), F32)] * 2,
        *[pltpu.VMEM((UNIT, UNIT), BF16)] * 8,
    ]


def pair_work(g):
    return [
        pltpu.VMEM((8, g), F32),
        pltpu.VMEM((g, 8), F32),
        *[pltpu.VMEM((G_ROWS, g), F32), pltpu.VMEM((H_ROWS, g), F32)] * 2,
        *[pltpu.VMEM((g, 4 * UNIT), BF16)] * 2,
    ]


def swap(block, axis, size, step):
    return lax.ppermute(block, axis, [(i, i ^ step) for i in range(size)])


def spread(block, axis, size):
    return [swap(block, axis, size, s) for s in range(size - 2, 0, -2)] + [block]


def local(n_row, n_col, positions, strengths, radii, pair_list, pair_count):
    g = radii.shape[0]
    part = g // 4
    hbm_spec = pl.BlockSpec(memory_space=pltpu.HBM)
    vmem_spec = pl.BlockSpec(memory_space=pltpu.VMEM)
    params = pltpu.CompilerParams(vmem_limit_bytes=VMEM)
    block = jax.ShapeDtypeStruct((8, g), F32)
    chunk = jax.ShapeDtypeStruct((6, part), F32)
    dense = jax.ShapeDtypeStruct((6 * g // 128, 128), F32)
    chunk_cost = pl.CostEstimate(flops=30 * g * part, bytes_accessed=64 * g, transcendentals=g * part)
    chunk_call = functools.partial(
        pl.pallas_call, scratch_shapes=own_work(part), compiler_params=params, cost_estimate=chunk_cost
    )

    def later(n, after):
        return chunk_call(
            functools.partial(later_kernel, n),
            out_shape=chunk,
            in_specs=[vmem_spec] * 7,
            out_specs=vmem_spec,
            name=f"own_{n}",
        )(pack, *common, after)

    pack = pl.pallas_call(
        pack_kernel,
        out_shape=block,
        in_specs=[hbm_spec] * 5,
        out_specs=vmem_spec,
        scratch_shapes=[
            pltpu.SMEM(pair_list.shape, jnp.int32),
            pltpu.SMEM(pair_count.shape, jnp.int32),
            pltpu.SemaphoreType.DMA((5,)),
        ],
        name="pack_group",
    )(positions, strengths, radii[None], pair_list, pair_count)

    own = []
    near_a, near_b = pack[None], pack[None]
    for stage in range(n_col.bit_length() - 1):
        step_a, step_b = n_col >> (1 + stage), n_row >> (1 + stage)
        far_a = swap(near_a, "col", n_col, step_a)
        if step_b:
            far_b = swap(near_b, "row", n_row, step_b)
        if step_a == 1:
            break
        if stage == 0:
            chunk_0, *common = chunk_call(
                first_kernel,
                out_shape=(
                    chunk,
                    jax.ShapeDtypeStruct((g, Q_ROWS), BF16),
                    jax.ShapeDtypeStruct((g, Q_ROWS), F32),
                    jax.ShapeDtypeStruct((Q_ROWS, g), BF16),
                    jax.ShapeDtypeStruct((G_ROWS, g), BF16),
                    jax.ShapeDtypeStruct((H_ROWS, g), BF16),
                ),
                in_specs=[vmem_spec],
                out_specs=(vmem_spec,) * 6,
                name="own_first",
            )(pack)
            own.append(chunk_0)
        elif stage == 1:
            own.append(later(1, near_a))
            own.append(later(2, near_a))
        arrived = own[-2:] + [far_b]
        runs = [(near_a, far_a)]
        if step_b > 1:
            runs.append((near_b, far_b))
        stacked = pl.pallas_call(
            functools.partial(stack_kernel, len(runs), len(arrived)),
            out_shape=tuple(jax.ShapeDtypeStruct((2 * n.shape[0], 8, g), F32) for n, _ in runs),
            in_specs=[vmem_spec] * (2 * len(runs) + len(arrived)),
            out_specs=(vmem_spec,) * len(runs),
            compiler_params=params,
            name="stack_groups",
        )(*[block for run in runs for block in run], *arrived)
        near_a = stacked[0]
        if len(runs) > 1:
            near_b = stacked[1]

    prepared = pl.pallas_call(
        prepare_kernel,
        out_shape=(
            block,
            block,
            jax.ShapeDtypeStruct((G_ROWS, g), BF16),
            jax.ShapeDtypeStruct((H_ROWS, g), BF16),
        ),
        in_specs=[vmem_spec] * 4,
        out_specs=(vmem_spec,) * 4,
        compiler_params=params,
        cost_estimate=pl.CostEstimate(flops=g * g, bytes_accessed=64 * g, transcendentals=0),
        name="prepare_group",
    )(pack, near_b, far_b, near_a)

    side_a, side_b = pl.pallas_call(
        pair_kernel,
        out_shape=(dense, dense),
        in_specs=[vmem_spec] * 8,
        out_specs=(vmem_spec, vmem_spec),
        scratch_shapes=pair_work(g),
        compiler_params=params,
        cost_estimate=pl.CostEstimate(flops=60 * g * g, bytes_accessed=128 * g, transcendentals=g * g),
        name="listed_pair",
    )(pack, near_a, far_a, *prepared, own[-1])

    def merge(parts, near, axis):
        return pl.pallas_call(
            functools.partial(merge_kernel, axis, len(parts)),
            out_shape=(dense,) * 2,
            in_specs=[vmem_spec] * (len(parts) + 1),
            out_specs=(vmem_spec,) * 2,
            compiler_params=params,
            name="merge_" + axis,
        )(*parts, near)

    parts_a = spread(side_a, "col", n_col)
    parts_b = spread(side_b, "row", n_row)
    keep_b, send_b = merge(parts_b, near_b, "row")
    far_b = swap(send_b, "row", n_row, 1)
    keep_a, send_a = merge(parts_a, near_a, "col")
    far_a = swap(send_a, "col", n_col, 1)
    own.append(later(3, keep_a))

    three = jax.ShapeDtypeStruct((3, g), F32)
    return pl.pallas_call(
        sum_kernel,
        out_shape=(three, three),
        in_specs=[vmem_spec] * 8,
        out_specs=(vmem_spec, vmem_spec),
        compiler_params=params,
        name="sum_parts",
    )(keep_a, keep_b, far_a, far_b, *own)


def solution(mesh):
    placed = (
        P(None, ("row", "col")),
        P(None, ("row", "col")),
        P(("row", "col")),
        P(None, "row", "col", None),
        P("row", "col"),
    )
    return jax.shard_map(
        functools.partial(local, mesh.shape["row"], mesh.shape["col"]),
        mesh=mesh,
        in_specs=placed,
        out_specs=(P(None, ("row", "col")), P(None, ("row", "col"))),
        check_vma=False,
    )
```

```python
import functools
import math

import jax
import jax.numpy as jnp
from jax import lax
from jax.experimental import pallas as pl
from jax.experimental.pallas import tpu as pltpu
from jax.sharding import PartitionSpec as P

F32 = jnp.float32
BF16 = jnp.bfloat16
UNIT = 256
STRIP = 16
G_ROWS = 32
H_ROWS = 96
Q_ROWS = 32
G_SCALE = -1.5 / (4.0 * math.pi)
H_SCALE = 7.5 / (4.0 * math.pi)
VMEM = 48 * 1024 * 1024


def cross(u, v):
    return jnp.concatenate(
        [
            u[1:2] * v[2:3] - u[2:3] * v[1:2],
            u[2:3] * v[0:1] - u[0:1] * v[2:3],
            u[0:1] * v[1:2] - u[1:2] * v[0:1],
        ]
    )


def split(f):
    hi = f.astype(BF16).astype(F32)
    mid = (f - hi).astype(BF16).astype(F32)
    return [hi, mid, (f - hi) - mid]


def features(pack):
    pos = pack[0:3] - 0.5
    st = pack[3:6]
    e0 = jnp.concatenate([st, cross(pos, st), jnp.zeros((2, pack.shape[1]), F32)])
    moments = jnp.concatenate([e0, pos[0:1] * e0, pos[1:2] * e0, pos[2:3] * e0])
    for_g = jnp.concatenate(split(e0) + [jnp.zeros_like(e0)]).astype(BF16)
    return for_g, jnp.concatenate(split(moments)).astype(BF16)


def widen(pack):
    for_g, for_h = features(pack)
    both = jnp.transpose(jnp.concatenate([for_h.astype(F32), for_g.astype(F32)]))
    at = lax.broadcasted_iota(jnp.int32, both.shape, 1)
    wide_g = jnp.where(at < H_ROWS, 0.0, both).astype(BF16)
    wide_h = jnp.where(at < H_ROWS, both, 0.0).astype(BF16)
    return wide_g, wide_h


def finish(pack, g, h):
    g = g[0:8] + g[8:16] + g[16:24]
    h = h[0:32] + h[32:64] + h[64:96]
    pos = pack[0:3] - 0.5
    st = pack[3:6]
    dot = jnp.sum(pos * st, axis=0, keepdims=True)
    d = dot * h[0:8] - st[0:1] * h[8:16] - st[1:2] * h[16:24] - st[2:3] * h[24:32]
    vel = G_SCALE * (cross(pos, g[0:3]) - g[3:6])
    stretch = G_SCALE * cross(st, g[0:3]) + H_SCALE * (cross(pos, d[0:3]) - d[3:6])
    return jnp.concatenate([vel, stretch])


def store_dense(out, value):
    rows = value.shape[0]
    for n in range(value.shape[1] // 128):
        out[n * rows : (n + 1) * rows, :] = value[:, n * 128 : (n + 1) * 128]


def load_dense(value, rows):
    return jnp.concatenate([value[n : n + rows] for n in range(0, value.shape[0], rows)], axis=1)


def strip(qq, s, images, r):
    ghi, glo, hhi, hlo = images
    here = slice(r, r + STRIP)
    t = lax.rsqrt(qq)
    t2 = t * t
    v = s * t2
    t3 = t2 * t
    g = t3 * (v + 2.0 / 3.0)
    h = (t3 * t2) * (v + 0.4)
    high = g.astype(BF16)
    ghi[here] = high
    glo[here] = (g - high.astype(F32)).astype(BF16)
    high = h.astype(BF16)
    hhi[here] = high
    hlo[here] = (h - high.astype(F32)).astype(BF16)


def down(f, image):
    return jnp.dot(f, image, preferred_element_type=F32)


def halves(pack):
    return 0.5 * pack[6:7] * pack[6:7]


def distances(pack):
    pos = pack[0:3] - 0.5
    x1, x2, x3 = split(pos)
    norm = jnp.concatenate(split(jnp.sum(pos * pos, axis=0, keepdims=True) + halves(pack)))
    one = jnp.ones_like(norm)
    blank = jnp.zeros((8, pack.shape[1]), F32)
    left = [-2.0 * x for x in (x1, x1, x2, x2, x1, x3)] + [norm, one, blank]
    right = [x1, x2, x1, x2, x3, x1, one, norm, blank]
    return jnp.concatenate(left), jnp.concatenate(right).astype(BF16)


def columns(pack, dist, s_col):
    left, right = distances(pack)
    blank = jnp.zeros((7, pack.shape[1]), F32)
    turned = jnp.transpose(jnp.concatenate([left[:24], halves(pack), blank]))
    s_col[...] = turned
    dist[...] = turned.astype(BF16)
    return right


def interact(dist_a, s_a, dist_b, s_b, feat_a, qq, slots, sums_b):
    for total in sums_b:
        total[...] = jnp.zeros_like(total)

    def products(i, j, images):
        pi, pj = slice(i, i + UNIT), slice(j, j + UNIT)
        steps = []

        def add(total, f, high, low):
            total[:, pj] += down(f, high[...]) + down(f, low[...])

        for kind in range(2):
            f = feat_a[kind][:, pi]
            steps.append(functools.partial(add, sums_b[kind], f, *images[2 * kind : 2 * kind + 2]))
        return steps

    def measure(unit, into):
        i, j = unit
        into[...] = down(dist_a[i : i + UNIT, :], dist_b[:, j : j + UNIT])

    n_strip = UNIT // STRIP
    units = [(i, j) for j in range(0, s_b.shape[1], UNIT) for i in range(0, s_a.shape[0], UNIT)]
    measure(units[0], qq[0])
    waiting = []
    for count, (i, j) in enumerate(units):
        images = slots[count % 2]
        if count + 1 < len(units):
            waiting.insert(0, functools.partial(measure, units[count + 1], qq[(count + 1) % 2]))
        per = n_strip // max(1, len(waiting))
        row = jnp.broadcast_to(s_b[0:1, j : j + UNIT], (STRIP, UNIT))
        for n in range(n_strip):
            at = slice(i + n * STRIP, i + (n + 1) * STRIP)
            here = slice(n * STRIP, (n + 1) * STRIP)
            strip(qq[count % 2][here, :], s_a[at, 24:25] + row, images, n * STRIP)
            if waiting and (n + 1) % per == 0:
                waiting.pop(0)()
        for step in waiting:
            step()
        waiting = products(i, j, images)
    for step in waiting:
        step()


def interact_both(dist_a, s_a, dist_b, s_b, feat_a, wide_b, qq, images, acc, sums_b):
    rows, n = s_a.shape[0], UNIT
    blocks, chunks = s_b.shape[1] // n, rows // n
    half = rows // 2

    def measure(block, c):
        here, part = slice(c * n, (c + 1) * n), slice(block * n, (block + 1) * n)
        qq[block % 2][here, :] = down(dist_a[here, :], dist_b[:, part])

    def onto_a(block, c):
        here, part = slice(c * n, (c + 1) * n), slice(block * n, (block + 1) * n)
        wide = jnp.concatenate([wide_b[0][part, :]] * 2 + [wide_b[1][part, :]] * 2)
        share = down(images[block % 2][here, :], wide)
        acc[here, :] = share if block == 0 else acc[here, :] + share

    def onto_b(block, later, kind):
        here, part = slice(later * half, (later + 1) * half), slice(block * n, (block + 1) * n)
        image = images[block % 2]
        at = 2 * kind * n
        f = feat_a[kind][:, here]
        share = down(f, image[here, at : at + n]) + down(f, image[here, at + n : at + 2 * n])
        sums_b[kind][:, part] = sums_b[kind][:, part] + share if later else share

    for c in range(chunks):
        measure(0, c)
    ready, delayed = [], []
    for block in range(blocks):
        image = images[block % 2]
        part = slice(block * n, (block + 1) * n)
        slots = [image.at[:, m * n : (m + 1) * n] for m in range(4)]
        row = jnp.broadcast_to(s_b[0:1, part], (STRIP, n))
        for c in range(chunks):
            todo, ready, delayed = ready, delayed, []
            if block + 1 < blocks:
                todo.append(functools.partial(measure, block + 1, c))
            n_strip = n // STRIP
            per = max(1, n_strip // max(1, len(todo)))
            for m in range(n_strip):
                here = slice(c * n + m * STRIP, c * n + (m + 1) * STRIP)
                strip(qq[block % 2][here, :], s_a[here, 24:25] + row, slots, c * n + m * STRIP)
                if todo and (m + 1) % per == 0:
                    todo.pop(0)()
            for step in todo:
                step()
            ready.append(functools.partial(onto_a, block, c))
            if (c + 1) % (chunks // 2) == 0:
                later = (c + 1) // (chunks // 2) - 1
                ready.append(functools.partial(onto_b, block, later, 0))
                delayed.append(functools.partial(onto_b, block, later, 1))
    for step in ready + delayed:
        step()


def own_chunk(n, pack, dist, s_col, right, feat, out, sums, qq, slots):
    part = slice(n * out.shape[1], (n + 1) * out.shape[1])
    interact(dist, s_col, right[:, part], halves(pack[:, part]), feat, qq, slots, sums)
    out[...] = finish(pack[:, part], sums[0][...], sums[1][...])


def first_kernel(pack, out, dist, s_col, right, feat_g, feat_h, b_g, b_h, *flat):
    right[...] = columns(pack[...], dist, s_col)
    feat_g[...], feat_h[...] = features(pack[...])
    own_chunk(0, pack, dist, s_col, right, (feat_g, feat_h), out, (b_g, b_h), flat[0:2], (flat[2:6], flat[6:10]))


def later_kernel(n, pack, dist, s_col, right, feat_g, feat_h, after, out, b_g, b_h, *flat):
    del after
    own_chunk(n, pack, dist, s_col, right, (feat_g, feat_h), out, (b_g, b_h), flat[0:2], (flat[2:6], flat[6:10]))


def pack_kernel(positions, strengths, radii, pair_list, pair_count, pack, listed, count, sems):
    copies = [
        pltpu.make_async_copy(pair_list, listed, sems.at[0]),
        pltpu.make_async_copy(pair_count, count, sems.at[1]),
        pltpu.make_async_copy(positions, pack.at[0:3], sems.at[2]),
        pltpu.make_async_copy(strengths, pack.at[3:6], sems.at[3]),
        pltpu.make_async_copy(radii, pack.at[6:7], sems.at[4]),
    ]
    for copy in copies:
        copy.start()
    for copy in copies[:2]:
        copy.wait()
    for n, value in enumerate((listed[0, 0, 0, 1], listed[1, 0, 0, 1], count[0, 0])):
        pack[7:8, n * 128 : (n + 1) * 128] = jnp.full((1, 128), value.astype(F32))
    rest = pack.shape[1] - 3 * 128
    pack[7:8, 3 * 128 :] = jnp.zeros((1, rest), F32)
    for copy in copies[2:]:
        copy.wait()


def here(axis):
    return lax.axis_index(axis).astype(jnp.int32)


def stack_kernel(n_pairs, n_arrived, *refs):
    del n_arrived
    for n in range(n_pairs):
        first, second, both = refs[2 * n], refs[2 * n + 1], refs[n - n_pairs]
        size = first.shape[0]
        both[0:size] = first[...]
        both[size : 2 * size] = second[...]


def place(relative, bits):
    at = 0
    for n in range(bits):
        at += ((relative >> n) & 1) << (bits - 1 - n)
    return at


def listed(pack):
    return [pack[7:8, n * 128 : (n + 1) * 128] for n in range(3)]


def choose(relative, near, far):
    at = place(relative >> 1, near.shape[0].bit_length() - 1)
    return jnp.where(relative % 2 == 0, near[at], far[at])


def prepare_kernel(pack, near, far, after, chosen, right, wide_g, wide_h):
    del after
    m = jnp.max(listed(pack)[1]).astype(jnp.int32)
    chosen[...] = choose(m ^ here("row"), near, far)
    right[...] = distances(chosen[...])[1]
    wide_g[...], wide_h[...] = widen(chosen[...])


def pair_kernel(pack, near, far, bpack, right, wide_g, wide_h, after, out_a, out_b, apack, dist, s_col, *rest):
    del after
    acc, sums_b, qq, images = rest[0], rest[1:3], rest[3:5], rest[5:7]
    k, _, count = [jnp.max(value).astype(jnp.int32) for value in listed(pack)]

    @pl.when(count > 1)
    def _():
        apack[...] = choose(k ^ here("col"), near, far)
        columns(apack[...], dist, s_col)
        feat_a = features(apack[...])
        interact_both(
            dist, s_col, right, halves(bpack[...]), feat_a, (wide_g, wide_h), qq, images, acc, sums_b
        )
        total = jnp.transpose(acc[...])
        store_dense(out_a, finish(apack[...], total[H_ROWS:], total[:H_ROWS]))
        store_dense(out_b, finish(bpack[...], sums_b[0][...], sums_b[1][...]))


def merge_kernel(axis, n_parts, *refs):
    parts, (near, keep, send) = refs[:n_parts], refs[n_parts:]
    at = here(axis)
    total = onward = jnp.zeros(keep.shape, F32)
    for n, part in enumerate(parts):
        relative = 2 * (n_parts - 1 - n)
        k, m, count = listed(near[place(relative >> 1, near.shape[0].bit_length() - 1)])
        if axis == "col":
            target = jnp.where(count > 1, k, -1.0)
        else:
            itself = (k == here("col").astype(F32)) & (m == (at ^ relative).astype(F32))
            target = jnp.where((count > 1) & ~itself, m, -1.0)
        block = part[...]
        total += jnp.where(target == at.astype(F32), block, 0.0)
        onward += jnp.where(target == (at ^ 1).astype(F32), block, 0.0)
    keep[...] = total
    send[...] = onward


def sum_kernel(keep_a, keep_b, part_a, part_b, *refs):
    own, (velocity, stretching) = refs[:-2], refs[-2:]
    total = load_dense(keep_a[...] + keep_b[...] + part_a[...] + part_b[...], 6)
    total += jnp.concatenate([chunk[...] for chunk in own], axis=1)
    velocity[...] = total[0:3]
    stretching[...] = total[3:6]


def own_work(cols):
    return [
        pltpu.VMEM((G_ROWS, cols), F32),
        pltpu.VMEM((H_ROWS, cols), F32),
        *[pltpu.VMEM((UNIT, UNIT), F32)] * 2,
        *[pltpu.VMEM((UNIT, UNIT), BF16)] * 8,
    ]


def pair_work(g):
    return [
        pltpu.VMEM((8, g), F32),
        pltpu.VMEM((g, Q_ROWS), BF16),
        pltpu.VMEM((g, Q_ROWS), F32),
        pltpu.VMEM((g, G_ROWS + H_ROWS), F32),
        pltpu.VMEM((G_ROWS, g), F32),
        pltpu.VMEM((H_ROWS, g), F32),
        *[pltpu.VMEM((g, UNIT), F32)] * 2,
        *[pltpu.VMEM((g, 4 * UNIT), BF16)] * 2,
    ]


def swap(block, axis, size, step):
    return lax.ppermute(block, axis, [(i, i ^ step) for i in range(size)])


def spread(block, axis, size):
    return [swap(block, axis, size, s) for s in range(size - 2, 0, -2)] + [block]


def local(n_row, n_col, positions, strengths, radii, pair_list, pair_count):
    g = radii.shape[0]
    part = g // 4
    hbm_spec = pl.BlockSpec(memory_space=pltpu.HBM)
    vmem_spec = pl.BlockSpec(memory_space=pltpu.VMEM)
    params = pltpu.CompilerParams(vmem_limit_bytes=VMEM)
    block = jax.ShapeDtypeStruct((8, g), F32)
    chunk = jax.ShapeDtypeStruct((6, part), F32)
    dense = jax.ShapeDtypeStruct((6 * g // 128, 128), F32)
    chunk_cost = pl.CostEstimate(flops=30 * g * part, bytes_accessed=64 * g, transcendentals=g * part)
    chunk_call = functools.partial(
        pl.pallas_call, scratch_shapes=own_work(part), compiler_params=params, cost_estimate=chunk_cost
    )

    def later(n, after):
        return chunk_call(
            functools.partial(later_kernel, n),
            out_shape=chunk,
            in_specs=[vmem_spec] * 7,
            out_specs=vmem_spec,
            name=f"own_{n}",
        )(pack, *common, after)

    pack = pl.pallas_call(
        pack_kernel,
        out_shape=block,
        in_specs=[hbm_spec] * 5,
        out_specs=vmem_spec,
        scratch_shapes=[
            pltpu.SMEM(pair_list.shape, jnp.int32),
            pltpu.SMEM(pair_count.shape, jnp.int32),
            pltpu.SemaphoreType.DMA((5,)),
        ],
        name="pack_group",
    )(positions, strengths, radii[None], pair_list, pair_count)

    own = []
    near_a, near_b = pack[None], pack[None]
    for stage in range(n_col.bit_length() - 1):
        step_a, step_b = n_col >> (1 + stage), n_row >> (1 + stage)
        far_a = swap(near_a, "col", n_col, step_a)
        if step_b:
            far_b = swap(near_b, "row", n_row, step_b)
        if step_a == 1:
            break
        if stage == 0:
            chunk_0, *common = chunk_call(
                first_kernel,
                out_shape=(
                    chunk,
                    jax.ShapeDtypeStruct((g, Q_ROWS), BF16),
                    jax.ShapeDtypeStruct((g, Q_ROWS), F32),
                    jax.ShapeDtypeStruct((Q_ROWS, g), BF16),
                    jax.ShapeDtypeStruct((G_ROWS, g), BF16),
                    jax.ShapeDtypeStruct((H_ROWS, g), BF16),
                ),
                in_specs=[vmem_spec],
                out_specs=(vmem_spec,) * 6,
                name="own_first",
            )(pack)
            own.append(chunk_0)
        elif stage == 1:
            own.append(later(1, near_a))
            own.append(later(2, near_a))
        arrived = own[-2:] + [far_b]
        runs = [(near_a, far_a)]
        if step_b > 1:
            runs.append((near_b, far_b))
        stacked = pl.pallas_call(
            functools.partial(stack_kernel, len(runs), len(arrived)),
            out_shape=tuple(jax.ShapeDtypeStruct((2 * n.shape[0], 8, g), F32) for n, _ in runs),
            in_specs=[vmem_spec] * (2 * len(runs) + len(arrived)),
            out_specs=(vmem_spec,) * len(runs),
            compiler_params=params,
            name="stack_groups",
        )(*[block for run in runs for block in run], *arrived)
        near_a = stacked[0]
        if len(runs) > 1:
            near_b = stacked[1]

    prepared = pl.pallas_call(
        prepare_kernel,
        out_shape=(
            block,
            jax.ShapeDtypeStruct((Q_ROWS, g), BF16),
            *[jax.ShapeDtypeStruct((g, G_ROWS + H_ROWS), BF16)] * 2,
        ),
        in_specs=[vmem_spec] * 4,
        out_specs=(vmem_spec,) * 4,
        compiler_params=params,
        cost_estimate=pl.CostEstimate(flops=g * g, bytes_accessed=64 * g, transcendentals=0),
        name="prepare_group",
    )(pack, near_b, far_b, near_a)

    side_a, side_b = pl.pallas_call(
        pair_kernel,
        out_shape=(dense, dense),
        in_specs=[vmem_spec] * 8,
        out_specs=(vmem_spec, vmem_spec),
        scratch_shapes=pair_work(g),
        compiler_params=params,
        cost_estimate=pl.CostEstimate(flops=60 * g * g, bytes_accessed=128 * g, transcendentals=g * g),
        name="listed_pair",
    )(pack, near_a, far_a, *prepared, own[-1])

    def merge(parts, near, axis):
        return pl.pallas_call(
            functools.partial(merge_kernel, axis, len(parts)),
            out_shape=(dense,) * 2,
            in_specs=[vmem_spec] * (len(parts) + 1),
            out_specs=(vmem_spec,) * 2,
            compiler_params=params,
            name="merge_" + axis,
        )(*parts, near)

    parts_a = spread(side_a, "col", n_col)
    parts_b = spread(side_b, "row", n_row)
    keep_b, send_b = merge(parts_b, near_b, "row")
    far_b = swap(send_b, "row", n_row, 1)
    keep_a, send_a = merge(parts_a, near_a, "col")
    far_a = swap(send_a, "col", n_col, 1)
    own.append(later(3, keep_a))

    three = jax.ShapeDtypeStruct((3, g), F32)
    return pl.pallas_call(
        sum_kernel,
        out_shape=(three, three),
        in_specs=[vmem_spec] * 8,
        out_specs=(vmem_spec, vmem_spec),
        compiler_params=params,
        name="sum_parts",
    )(keep_a, keep_b, far_a, far_b, *own)


def solution(mesh):
    placed = (
        P(None, ("row", "col")),
        P(None, ("row", "col")),
        P(("row", "col")),
        P(None, "row", "col", None),
        P("row", "col"),
    )
    return jax.shard_map(
        functools.partial(local, mesh.shape["row"], mesh.shape["col"]),
        mesh=mesh,
        in_specs=placed,
        out_specs=(P(None, ("row", "col")), P(None, ("row", "col"))),
        check_vma=False,
    )
```

```python
import functools
import math

import jax
import jax.numpy as jnp
from jax import lax
from jax.experimental import pallas as pl
from jax.experimental.pallas import tpu as pltpu
from jax.sharding import PartitionSpec as P

F32 = jnp.float32
BF16 = jnp.bfloat16
UNIT = 256
STRIP = 32
G_ROWS = 32
H_ROWS = 96
Q_ROWS = 32
G_SCALE = -1.5 / (4.0 * math.pi)
H_SCALE = 7.5 / (4.0 * math.pi)
VMEM = 48 * 1024 * 1024


def cross(u, v):
    return jnp.concatenate(
        [
            u[1:2] * v[2:3] - u[2:3] * v[1:2],
            u[2:3] * v[0:1] - u[0:1] * v[2:3],
            u[0:1] * v[1:2] - u[1:2] * v[0:1],
        ]
    )


def split(f):
    hi = f.astype(BF16).astype(F32)
    mid = (f - hi).astype(BF16).astype(F32)
    return [hi, mid, (f - hi) - mid]


def features(pack):
    pos = pack[0:3] - 0.5
    st = pack[3:6]
    e0 = jnp.concatenate([st, cross(pos, st), jnp.zeros((2, pack.shape[1]), F32)])
    moments = jnp.concatenate([e0, pos[0:1] * e0, pos[1:2] * e0, pos[2:3] * e0])
    for_g = jnp.concatenate(split(e0) + [jnp.zeros_like(e0)]).astype(BF16)
    return for_g, jnp.concatenate(split(moments)).astype(BF16)


def widen(pack):
    for_g, for_h = features(pack)
    both = jnp.transpose(jnp.concatenate([for_h.astype(F32), for_g.astype(F32)]))
    at = lax.broadcasted_iota(jnp.int32, both.shape, 1)
    wide_g = jnp.where(at < H_ROWS, 0.0, both).astype(BF16)
    wide_h = jnp.where(at < H_ROWS, both, 0.0).astype(BF16)
    return wide_g, wide_h


def finish(pack, g, h):
    g = g[0:8] + g[8:16] + g[16:24]
    h = h[0:32] + h[32:64] + h[64:96]
    pos = pack[0:3] - 0.5
    st = pack[3:6]
    dot = jnp.sum(pos * st, axis=0, keepdims=True)
    d = dot * h[0:8] - st[0:1] * h[8:16] - st[1:2] * h[16:24] - st[2:3] * h[24:32]
    vel = G_SCALE * (cross(pos, g[0:3]) - g[3:6])
    stretch = G_SCALE * cross(st, g[0:3]) + H_SCALE * (cross(pos, d[0:3]) - d[3:6])
    return jnp.concatenate([vel, stretch])


def store_dense(out, value):
    rows = value.shape[0]
    for n in range(value.shape[1] // 128):
        out[n * rows : (n + 1) * rows, :] = value[:, n * 128 : (n + 1) * 128]


def load_dense(value, rows):
    return jnp.concatenate([value[n : n + rows] for n in range(0, value.shape[0], rows)], axis=1)


def strip(qq, s, images, r):
    ghi, glo, hhi, hlo = images
    here = slice(r, r + STRIP)
    t = lax.rsqrt(qq)
    t2 = t * t
    v = s * t2
    t3 = t2 * t
    g = t3 * (v + 2.0 / 3.0)
    h = (t3 * t2) * (v + 0.4)
    high = g.astype(BF16)
    ghi[here] = high
    glo[here] = (g - high.astype(F32)).astype(BF16)
    high = h.astype(BF16)
    hhi[here] = high
    hlo[here] = (h - high.astype(F32)).astype(BF16)


def down(f, image):
    return jnp.dot(f, image, preferred_element_type=F32)


def halves(pack):
    return 0.5 * pack[6:7] * pack[6:7]


def distances(pack):
    pos = pack[0:3] - 0.5
    x1, x2, x3 = split(pos)
    norm = jnp.concatenate(split(jnp.sum(pos * pos, axis=0, keepdims=True) + halves(pack)))
    one = jnp.ones_like(norm)
    blank = jnp.zeros((8, pack.shape[1]), F32)
    left = [-2.0 * x for x in (x1, x1, x2, x2, x1, x3)] + [norm, one, blank]
    right = [x1, x2, x1, x2, x3, x1, one, norm, blank]
    return jnp.concatenate(left), jnp.concatenate(right).astype(BF16)


def columns(pack, dist, s_col):
    left, right = distances(pack)
    blank = jnp.zeros((7, pack.shape[1]), F32)
    turned = jnp.transpose(jnp.concatenate([left[:24], halves(pack), blank]))
    s_col[...] = turned
    dist[...] = turned.astype(BF16)
    return right


def interact(dist_a, s_a, dist_b, s_b, feat_a, qq, slots, sums_b):
    for total in sums_b:
        total[...] = jnp.zeros_like(total)

    def products(i, j, images):
        pi, pj = slice(i, i + UNIT), slice(j, j + UNIT)
        steps = []

        def add(total, f, high, low):
            total[:, pj] += down(f, high[...]) + down(f, low[...])

        for kind in range(2):
            f = feat_a[kind][:, pi]
            steps.append(functools.partial(add, sums_b[kind], f, *images[2 * kind : 2 * kind + 2]))
        return steps

    def measure(unit, into):
        i, j = unit
        into[...] = down(dist_a[i : i + UNIT, :], dist_b[:, j : j + UNIT])

    n_strip = UNIT // STRIP
    units = [(i, j) for j in range(0, s_b.shape[1], UNIT) for i in range(0, s_a.shape[0], UNIT)]
    measure(units[0], qq[0])
    waiting = []
    for count, (i, j) in enumerate(units):
        images = slots[count % 2]
        if count + 1 < len(units):
            waiting.insert(0, functools.partial(measure, units[count + 1], qq[(count + 1) % 2]))
        per = n_strip // max(1, len(waiting))
        row = jnp.broadcast_to(s_b[0:1, j : j + UNIT], (STRIP, UNIT))
        for n in range(n_strip):
            at = slice(i + n * STRIP, i + (n + 1) * STRIP)
            here = slice(n * STRIP, (n + 1) * STRIP)
            strip(qq[count % 2][here, :], s_a[at, 24:25] + row, images, n * STRIP)
            if waiting and (n + 1) % per == 0:
                waiting.pop(0)()
        for step in waiting:
            step()
        waiting = products(i, j, images)
    for step in waiting:
        step()


def interact_both(dist_a, s_a, dist_b, s_b, feat_a, wide_b, qq, images, acc, sums_b):
    rows, n = s_a.shape[0], UNIT
    blocks, chunks = s_b.shape[1] // n, rows // n
    half = rows // 2

    def measure(block, c):
        here, part = slice(c * n, (c + 1) * n), slice(block * n, (block + 1) * n)
        qq[block % 2][here, :] = down(dist_a[here, :], dist_b[:, part])

    def onto_a(block, c):
        here, part = slice(c * n, (c + 1) * n), slice(block * n, (block + 1) * n)
        wide = jnp.concatenate([wide_b[0][part, :]] * 2 + [wide_b[1][part, :]] * 2)
        share = down(images[block % 2][here, :], wide)
        acc[here, :] = share if block == 0 else acc[here, :] + share

    def onto_b(block, later, kind):
        here, part = slice(later * half, (later + 1) * half), slice(block * n, (block + 1) * n)
        image = images[block % 2]
        at = 2 * kind * n
        f = feat_a[kind][:, here]
        share = down(f, image[here, at : at + n]) + down(f, image[here, at + n : at + 2 * n])
        sums_b[kind][:, part] = sums_b[kind][:, part] + share if later else share

    for c in range(chunks):
        measure(0, c)
    ready, delayed = [], []
    for block in range(blocks):
        image = images[block % 2]
        part = slice(block * n, (block + 1) * n)
        slots = [image.at[:, m * n : (m + 1) * n] for m in range(4)]
        row = jnp.broadcast_to(s_b[0:1, part], (STRIP, n))
        for c in range(chunks):
            todo, ready, delayed = ready, delayed, []
            if block + 1 < blocks:
                todo.append(functools.partial(measure, block + 1, c))
            n_strip = n // STRIP
            per = max(1, n_strip // max(1, len(todo)))
            for m in range(n_strip):
                here = slice(c * n + m * STRIP, c * n + (m + 1) * STRIP)
                strip(qq[block % 2][here, :], s_a[here, 24:25] + row, slots, c * n + m * STRIP)
                if todo and (m + 1) % per == 0:
                    todo.pop(0)()
            for step in todo:
                step()
            ready.append(functools.partial(onto_a, block, c))
            if (c + 1) % (chunks // 2) == 0:
                later = (c + 1) // (chunks // 2) - 1
                ready.append(functools.partial(onto_b, block, later, 0))
                delayed.append(functools.partial(onto_b, block, later, 1))
    for step in ready + delayed:
        step()


def own_chunk(n, pack, dist, s_col, right, feat, out, sums, qq, slots):
    part = slice(n * out.shape[1], (n + 1) * out.shape[1])
    interact(dist, s_col, right[:, part], halves(pack[:, part]), feat, qq, slots, sums)
    out[...] = finish(pack[:, part], sums[0][...], sums[1][...])


def first_kernel(pack, out, dist, s_col, right, feat_g, feat_h, b_g, b_h, *flat):
    right[...] = columns(pack[...], dist, s_col)
    feat_g[...], feat_h[...] = features(pack[...])
    own_chunk(0, pack, dist, s_col, right, (feat_g, feat_h), out, (b_g, b_h), flat[0:2], (flat[2:6], flat[6:10]))


def later_kernel(n, pack, dist, s_col, right, feat_g, feat_h, after, out, b_g, b_h, *flat):
    del after
    own_chunk(n, pack, dist, s_col, right, (feat_g, feat_h), out, (b_g, b_h), flat[0:2], (flat[2:6], flat[6:10]))


def pack_kernel(positions, strengths, radii, pair_list, pair_count, pack, listed, count, sems):
    copies = [
        pltpu.make_async_copy(pair_list, listed, sems.at[0]),
        pltpu.make_async_copy(pair_count, count, sems.at[1]),
        pltpu.make_async_copy(positions, pack.at[0:3], sems.at[2]),
        pltpu.make_async_copy(strengths, pack.at[3:6], sems.at[3]),
        pltpu.make_async_copy(radii, pack.at[6:7], sems.at[4]),
    ]
    for copy in copies:
        copy.start()
    for copy in copies[:2]:
        copy.wait()
    for n, value in enumerate((listed[0, 0, 0, 1], listed[1, 0, 0, 1], count[0, 0])):
        pack[7:8, n * 128 : (n + 1) * 128] = jnp.full((1, 128), value.astype(F32))
    rest = pack.shape[1] - 3 * 128
    pack[7:8, 3 * 128 :] = jnp.zeros((1, rest), F32)
    for copy in copies[2:]:
        copy.wait()


def here(axis):
    return lax.axis_index(axis).astype(jnp.int32)


def stack_kernel(n_pairs, n_arrived, *refs):
    del n_arrived
    for n in range(n_pairs):
        first, second, both = refs[2 * n], refs[2 * n + 1], refs[n - n_pairs]
        size = first.shape[0]
        both[0:size] = first[...]
        both[size : 2 * size] = second[...]


def place(relative, bits):
    at = 0
    for n in range(bits):
        at += ((relative >> n) & 1) << (bits - 1 - n)
    return at


def listed(pack):
    return [pack[7:8, n * 128 : (n + 1) * 128] for n in range(3)]


def choose(relative, near, far):
    at = place(relative >> 1, near.shape[0].bit_length() - 1)
    return jnp.where(relative % 2 == 0, near[at], far[at])


def prepare_kernel(pack, near, far, after, chosen, right, wide_g, wide_h):
    del after
    m = jnp.max(listed(pack)[1]).astype(jnp.int32)
    chosen[...] = choose(m ^ here("row"), near, far)
    right[...] = distances(chosen[...])[1]
    wide_g[...], wide_h[...] = widen(chosen[...])


def pair_kernel(pack, near, far, bpack, right, wide_g, wide_h, after, out_a, out_b, apack, dist, s_col, *rest):
    del after
    acc, sums_b, qq, images = rest[0], rest[1:3], rest[3:5], rest[5:7]
    k, _, count = [jnp.max(value).astype(jnp.int32) for value in listed(pack)]

    @pl.when(count > 1)
    def _():
        apack[...] = choose(k ^ here("col"), near, far)
        columns(apack[...], dist, s_col)
        feat_a = features(apack[...])
        interact_both(
            dist, s_col, right, halves(bpack[...]), feat_a, (wide_g, wide_h), qq, images, acc, sums_b
        )
        total = jnp.transpose(acc[...])
        store_dense(out_a, finish(apack[...], total[H_ROWS:], total[:H_ROWS]))
        store_dense(out_b, finish(bpack[...], sums_b[0][...], sums_b[1][...]))


def merge_kernel(axis, n_parts, *refs):
    parts, (near, keep, send) = refs[:n_parts], refs[n_parts:]
    at = here(axis)
    total = onward = jnp.zeros(keep.shape, F32)
    for n, part in enumerate(parts):
        relative = 2 * (n_parts - 1 - n)
        k, m, count = listed(near[place(relative >> 1, near.shape[0].bit_length() - 1)])
        if axis == "col":
            target = jnp.where(count > 1, k, -1.0)
        else:
            itself = (k == here("col").astype(F32)) & (m == (at ^ relative).astype(F32))
            target = jnp.where((count > 1) & ~itself, m, -1.0)
        block = part[...]
        total += jnp.where(target == at.astype(F32), block, 0.0)
        onward += jnp.where(target == (at ^ 1).astype(F32), block, 0.0)
    keep[...] = total
    send[...] = onward


def sum_kernel(keep_a, keep_b, part_a, part_b, *refs):
    own, (velocity, stretching) = refs[:-2], refs[-2:]
    total = load_dense(keep_a[...] + keep_b[...] + part_a[...] + part_b[...], 6)
    total += jnp.concatenate([chunk[...] for chunk in own], axis=1)
    velocity[...] = total[0:3]
    stretching[...] = total[3:6]


def own_work(cols):
    return [
        pltpu.VMEM((G_ROWS, cols), F32),
        pltpu.VMEM((H_ROWS, cols), F32),
        *[pltpu.VMEM((UNIT, UNIT), F32)] * 2,
        *[pltpu.VMEM((UNIT, UNIT), BF16)] * 8,
    ]


def pair_work(g):
    return [
        pltpu.VMEM((8, g), F32),
        pltpu.VMEM((g, Q_ROWS), BF16),
        pltpu.VMEM((g, Q_ROWS), F32),
        pltpu.VMEM((g, G_ROWS + H_ROWS), F32),
        pltpu.VMEM((G_ROWS, g), F32),
        pltpu.VMEM((H_ROWS, g), F32),
        *[pltpu.VMEM((g, UNIT), F32)] * 2,
        *[pltpu.VMEM((g, 4 * UNIT), BF16)] * 2,
    ]


def swap(block, axis, size, step):
    return lax.ppermute(block, axis, [(i, i ^ step) for i in range(size)])


def spread(block, axis, size):
    return [swap(block, axis, size, s) for s in range(size - 2, 0, -2)] + [block]


def local(n_row, n_col, positions, strengths, radii, pair_list, pair_count):
    g = radii.shape[0]
    part = g // 4
    hbm_spec = pl.BlockSpec(memory_space=pltpu.HBM)
    vmem_spec = pl.BlockSpec(memory_space=pltpu.VMEM)
    params = pltpu.CompilerParams(vmem_limit_bytes=VMEM)
    block = jax.ShapeDtypeStruct((8, g), F32)
    chunk = jax.ShapeDtypeStruct((6, part), F32)
    dense = jax.ShapeDtypeStruct((6 * g // 128, 128), F32)
    chunk_cost = pl.CostEstimate(flops=30 * g * part, bytes_accessed=64 * g, transcendentals=g * part)
    chunk_call = functools.partial(
        pl.pallas_call, scratch_shapes=own_work(part), compiler_params=params, cost_estimate=chunk_cost
    )

    def later(n, after):
        return chunk_call(
            functools.partial(later_kernel, n),
            out_shape=chunk,
            in_specs=[vmem_spec] * 7,
            out_specs=vmem_spec,
            name=f"own_{n}",
        )(pack, *common, after)

    pack = pl.pallas_call(
        pack_kernel,
        out_shape=block,
        in_specs=[hbm_spec] * 5,
        out_specs=vmem_spec,
        scratch_shapes=[
            pltpu.SMEM(pair_list.shape, jnp.int32),
            pltpu.SMEM(pair_count.shape, jnp.int32),
            pltpu.SemaphoreType.DMA((5,)),
        ],
        name="pack_group",
    )(positions, strengths, radii[None], pair_list, pair_count)

    own = []
    near_a, near_b = pack[None], pack[None]
    for stage in range(n_col.bit_length() - 1):
        step_a, step_b = n_col >> (1 + stage), n_row >> (1 + stage)
        far_a = swap(near_a, "col", n_col, step_a)
        if step_b:
            far_b = swap(near_b, "row", n_row, step_b)
        if step_a == 1:
            break
        if stage == 0:
            chunk_0, *common = chunk_call(
                first_kernel,
                out_shape=(
                    chunk,
                    jax.ShapeDtypeStruct((g, Q_ROWS), BF16),
                    jax.ShapeDtypeStruct((g, Q_ROWS), F32),
                    jax.ShapeDtypeStruct((Q_ROWS, g), BF16),
                    jax.ShapeDtypeStruct((G_ROWS, g), BF16),
                    jax.ShapeDtypeStruct((H_ROWS, g), BF16),
                ),
                in_specs=[vmem_spec],
                out_specs=(vmem_spec,) * 6,
                name="own_first",
            )(pack)
            own.append(chunk_0)
        elif stage == 1:
            own.append(later(1, near_a))
            own.append(later(2, near_a))
        arrived = own[-2:] + [far_b]
        runs = [(near_a, far_a)]
        if step_b > 1:
            runs.append((near_b, far_b))
        stacked = pl.pallas_call(
            functools.partial(stack_kernel, len(runs), len(arrived)),
            out_shape=tuple(jax.ShapeDtypeStruct((2 * n.shape[0], 8, g), F32) for n, _ in runs),
            in_specs=[vmem_spec] * (2 * len(runs) + len(arrived)),
            out_specs=(vmem_spec,) * len(runs),
            compiler_params=params,
            name="stack_groups",
        )(*[block for run in runs for block in run], *arrived)
        near_a = stacked[0]
        if len(runs) > 1:
            near_b = stacked[1]

    prepared = pl.pallas_call(
        prepare_kernel,
        out_shape=(
            block,
            jax.ShapeDtypeStruct((Q_ROWS, g), BF16),
            *[jax.ShapeDtypeStruct((g, G_ROWS + H_ROWS), BF16)] * 2,
        ),
        in_specs=[vmem_spec] * 4,
        out_specs=(vmem_spec,) * 4,
        compiler_params=params,
        cost_estimate=pl.CostEstimate(flops=g * g, bytes_accessed=64 * g, transcendentals=0),
        name="prepare_group",
    )(pack, near_b, far_b, near_a)

    side_a, side_b = pl.pallas_call(
        pair_kernel,
        out_shape=(dense, dense),
        in_specs=[vmem_spec] * 8,
        out_specs=(vmem_spec, vmem_spec),
        scratch_shapes=pair_work(g),
        compiler_params=params,
        cost_estimate=pl.CostEstimate(flops=60 * g * g, bytes_accessed=128 * g, transcendentals=g * g),
        name="listed_pair",
    )(pack, near_a, far_a, *prepared, own[-1])

    def merge(parts, near, axis):
        return pl.pallas_call(
            functools.partial(merge_kernel, axis, len(parts)),
            out_shape=(dense,) * 2,
            in_specs=[vmem_spec] * (len(parts) + 1),
            out_specs=(vmem_spec,) * 2,
            compiler_params=params,
            name="merge_" + axis,
        )(*parts, near)

    parts_a = spread(side_a, "col", n_col)
    parts_b = spread(side_b, "row", n_row)
    keep_b, send_b = merge(parts_b, near_b, "row")
    far_b = swap(send_b, "row", n_row, 1)
    keep_a, send_a = merge(parts_a, near_a, "col")
    far_a = swap(send_a, "col", n_col, 1)
    own.append(later(3, keep_a))

    three = jax.ShapeDtypeStruct((3, g), F32)
    return pl.pallas_call(
        sum_kernel,
        out_shape=(three, three),
        in_specs=[vmem_spec] * 8,
        out_specs=(vmem_spec, vmem_spec),
        compiler_params=params,
        name="sum_parts",
    )(keep_a, keep_b, far_a, far_b, *own)


def solution(mesh):
    placed = (
        P(None, ("row", "col")),
        P(None, ("row", "col")),
        P(("row", "col")),
        P(None, "row", "col", None),
        P("row", "col"),
    )
    return jax.shard_map(
        functools.partial(local, mesh.shape["row"], mesh.shape["col"]),
        mesh=mesh,
        in_specs=placed,
        out_specs=(P(None, ("row", "col")), P(None, ("row", "col"))),
        check_vma=False,
    )
```

```python
import functools
import math

import jax
import jax.numpy as jnp
from jax import lax
from jax.experimental import pallas as pl
from jax.experimental.pallas import tpu as pltpu
from jax.sharding import PartitionSpec as P

F32 = jnp.float32
BF16 = jnp.bfloat16
UNIT = 256
STRIP = 16
G_ROWS = 32
H_ROWS = 96
Q_ROWS = 32
G_SCALE = -1.5 / (4.0 * math.pi)
H_SCALE = 7.5 / (4.0 * math.pi)
VMEM = 48 * 1024 * 1024


def cross(u, v):
    return jnp.concatenate(
        [
            u[1:2] * v[2:3] - u[2:3] * v[1:2],
            u[2:3] * v[0:1] - u[0:1] * v[2:3],
            u[0:1] * v[1:2] - u[1:2] * v[0:1],
        ]
    )


def split(f):
    hi = f.astype(BF16).astype(F32)
    mid = (f - hi).astype(BF16).astype(F32)
    return [hi, mid, (f - hi) - mid]


def features(pack):
    pos = pack[0:3] - 0.5
    st = pack[3:6]
    e0 = jnp.concatenate([st, cross(pos, st), jnp.zeros((2, pack.shape[1]), F32)])
    moments = jnp.concatenate([e0, pos[0:1] * e0, pos[1:2] * e0, pos[2:3] * e0])
    for_g = jnp.concatenate(split(e0) + [jnp.zeros_like(e0)]).astype(BF16)
    return for_g, jnp.concatenate(split(moments)).astype(BF16)


def finish(pack, g, h):
    g = g[0:8] + g[8:16] + g[16:24]
    h = h[0:32] + h[32:64] + h[64:96]
    pos = pack[0:3] - 0.5
    st = pack[3:6]
    dot = jnp.sum(pos * st, axis=0, keepdims=True)
    d = dot * h[0:8] - st[0:1] * h[8:16] - st[1:2] * h[16:24] - st[2:3] * h[24:32]
    vel = G_SCALE * (cross(pos, g[0:3]) - g[3:6])
    stretch = G_SCALE * cross(st, g[0:3]) + H_SCALE * (cross(pos, d[0:3]) - d[3:6])
    return jnp.concatenate([vel, stretch])


def store_dense(out, value):
    rows = value.shape[0]
    for n in range(value.shape[1] // 128):
        out[n * rows : (n + 1) * rows, :] = value[:, n * 128 : (n + 1) * 128]


def load_dense(value, rows):
    return jnp.concatenate([value[n : n + rows] for n in range(0, value.shape[0], rows)], axis=1)


def strip(qq, s, images, r):
    ghi, glo, hhi, hlo = images
    here = slice(r, r + STRIP)
    t = lax.rsqrt(qq)
    t2 = t * t
    v = s * t2
    t3 = t2 * t
    g = t3 * (v + 2.0 / 3.0)
    h = (t3 * t2) * (v + 0.4)
    high = g.astype(BF16)
    ghi[here] = high
    glo[here] = (g - high.astype(F32)).astype(BF16)
    high = h.astype(BF16)
    hhi[here] = high
    hlo[here] = (h - high.astype(F32)).astype(BF16)


def down(f, image):
    return jnp.dot(f, image, preferred_element_type=F32)


def across(f, image):
    return lax.dot_general(f, image, (((1,), (1,)), ((), ())), preferred_element_type=F32)


def halves(pack):
    return 0.5 * pack[6:7] * pack[6:7]


def distances(pack):
    pos = pack[0:3] - 0.5
    x1, x2, x3 = split(pos)
    norm = jnp.concatenate(split(jnp.sum(pos * pos, axis=0, keepdims=True) + halves(pack)))
    one = jnp.ones_like(norm)
    blank = jnp.zeros((8, pack.shape[1]), F32)
    left = [-2.0 * x for x in (x1, x1, x2, x2, x1, x3)] + [norm, one, blank]
    right = [x1, x2, x1, x2, x3, x1, one, norm, blank]
    return jnp.concatenate(left), jnp.concatenate(right).astype(BF16)


def columns(pack, dist, s_col):
    left, right = distances(pack)
    blank = jnp.zeros((7, pack.shape[1]), F32)
    turned = jnp.transpose(jnp.concatenate([left[:24], halves(pack), blank]))
    s_col[...] = turned
    dist[...] = turned.astype(BF16)
    return right


def outline(pack, factor):
    pos = pack[0:3] - 0.5
    half = halves(pack)
    norm = jnp.sum(pos * pos, axis=0, keepdims=True) + half
    return jnp.concatenate([factor * pos, norm, half, jnp.zeros((3, pack.shape[1]), F32)])


def interact(dist_a, s_a, dist_b, s_b, feat_a, qq, slots, sums_b):
    for total in sums_b:
        total[...] = jnp.zeros_like(total)

    def products(i, j, images):
        pi, pj = slice(i, i + UNIT), slice(j, j + UNIT)
        steps = []

        def add(total, f, high, low):
            total[:, pj] += down(f, high[...]) + down(f, low[...])

        for kind in range(2):
            f = feat_a[kind][:, pi]
            steps.append(functools.partial(add, sums_b[kind], f, *images[2 * kind : 2 * kind + 2]))
        return steps

    def measure(unit, into):
        i, j = unit
        into[...] = down(dist_a[i : i + UNIT, :], dist_b[:, j : j + UNIT])

    n_strip = UNIT // STRIP
    units = [(i, j) for j in range(0, s_b.shape[1], UNIT) for i in range(0, s_a.shape[0], UNIT)]
    measure(units[0], qq[0])
    waiting = []
    for count, (i, j) in enumerate(units):
        images = slots[count % 2]
        if count + 1 < len(units):
            waiting.insert(0, functools.partial(measure, units[count + 1], qq[(count + 1) % 2]))
        per = n_strip // max(1, len(waiting))
        row = jnp.broadcast_to(s_b[0:1, j : j + UNIT], (STRIP, UNIT))
        for n in range(n_strip):
            at = slice(i + n * STRIP, i + (n + 1) * STRIP)
            here = slice(n * STRIP, (n + 1) * STRIP)
            strip(qq[count % 2][here, :], s_a[at, 24:25] + row, images, n * STRIP)
            if waiting and (n + 1) % per == 0:
                waiting.pop(0)()
        for step in waiting:
            step()
        waiting = products(i, j, images)
    for step in waiting:
        step()


def interact_both(col, spread_col, rows_b, feat_a, feat_b, images, sums_a, sums_b):
    rows, n = col.shape[0], UNIT
    blocks, chunks = rows_b.shape[1] // n, rows // n
    half = rows // 2

    def onto_a(block, c, kind):
        here, part = slice(c * n, (c + 1) * n), slice(block * n, (block + 1) * n)
        f = jnp.concatenate([feat_b[kind][:, part]] * 2, axis=1)
        share = across(f, images[block % 2][here, 2 * kind * n : 2 * (kind + 1) * n])
        sums_a[kind][:, here] = share if block == 0 else sums_a[kind][:, here] + share

    def onto_b(block, later, kind):
        here, part = slice(later * half, (later + 1) * half), slice(block * n, (block + 1) * n)
        image = images[block % 2]
        at = 2 * kind * n
        f = jnp.concatenate([feat_a[kind][:, here]] * 2, axis=1)
        share = down(f, jnp.concatenate([image[here, at : at + n], image[here, at + n : at + 2 * n]]))
        sums_b[kind][:, part] = sums_b[kind][:, part] + share if later else share

    ready, delayed = [], []
    for block in range(blocks):
        image = images[block % 2]
        part = slice(block * n, (block + 1) * n)
        slots = [image.at[:, m * n : (m + 1) * n] for m in range(4)]
        row = [jnp.broadcast_to(rows_b[m : m + 1, part], (STRIP, n)) for m in range(5)]
        for c in range(chunks):
            todo, ready, delayed = ready, delayed, []
            n_strip = n // STRIP
            per = max(1, n_strip // max(1, len(todo)))
            for m in range(n_strip):
                here = slice(c * n + m * STRIP, c * n + (m + 1) * STRIP)
                own = []
                for q in range(5):
                    if block == 0:
                        spread_col[q, here, :] = jnp.broadcast_to(col[here, q : q + 1], (STRIP, 128))
                    own.append(jnp.concatenate([spread_col[q, here, :]] * (n // 128), axis=1))
                qq = own[0] * row[0] + own[1] * row[1] + own[2] * row[2] + (own[3] + row[3])
                strip(qq, own[4] + row[4], slots, c * n + m * STRIP)
                if todo and (m + 1) % per == 0:
                    todo.pop(0)()
            for step in todo:
                step()
            for kind in range(2):
                ready.append(functools.partial(onto_a, block, c, kind))
            if (c + 1) % (chunks // 2) == 0:
                later = (c + 1) // (chunks // 2) - 1
                ready.append(functools.partial(onto_b, block, later, 0))
                delayed.append(functools.partial(onto_b, block, later, 1))
    for step in ready + delayed:
        step()


def own_chunk(n, pack, dist, s_col, right, feat, out, sums, qq, slots):
    part = slice(n * out.shape[1], (n + 1) * out.shape[1])
    interact(dist, s_col, right[:, part], halves(pack[:, part]), feat, qq, slots, sums)
    out[...] = finish(pack[:, part], sums[0][...], sums[1][...])


def first_kernel(pack, out, dist, s_col, right, feat_g, feat_h, b_g, b_h, *flat):
    right[...] = columns(pack[...], dist, s_col)
    feat_g[...], feat_h[...] = features(pack[...])
    own_chunk(0, pack, dist, s_col, right, (feat_g, feat_h), out, (b_g, b_h), flat[0:2], (flat[2:6], flat[6:10]))


def later_kernel(n, pack, dist, s_col, right, feat_g, feat_h, after, out, b_g, b_h, *flat):
    del after
    own_chunk(n, pack, dist, s_col, right, (feat_g, feat_h), out, (b_g, b_h), flat[0:2], (flat[2:6], flat[6:10]))


def pack_kernel(positions, strengths, radii, pair_list, pair_count, pack, listed, count, sems):
    copies = [
        pltpu.make_async_copy(pair_list, listed, sems.at[0]),
        pltpu.make_async_copy(pair_count, count, sems.at[1]),
        pltpu.make_async_copy(positions, pack.at[0:3], sems.at[2]),
        pltpu.make_async_copy(strengths, pack.at[3:6], sems.at[3]),
        pltpu.make_async_copy(radii, pack.at[6:7], sems.at[4]),
    ]
    for copy in copies:
        copy.start()
    for copy in copies[:2]:
        copy.wait()
    for n, value in enumerate((listed[0, 0, 0, 1], listed[1, 0, 0, 1], count[0, 0])):
        pack[7:8, n * 128 : (n + 1) * 128] = jnp.full((1, 128), value.astype(F32))
    rest = pack.shape[1] - 3 * 128
    pack[7:8, 3 * 128 :] = jnp.zeros((1, rest), F32)
    for copy in copies[2:]:
        copy.wait()


def here(axis):
    return lax.axis_index(axis).astype(jnp.int32)


def stack_kernel(n_pairs, n_arrived, *refs):
    del n_arrived
    for n in range(n_pairs):
        first, second, both = refs[2 * n], refs[2 * n + 1], refs[n - n_pairs]
        size = first.shape[0]
        both[0:size] = first[...]
        both[size : 2 * size] = second[...]


def place(relative, bits):
    at = 0
    for n in range(bits):
        at += ((relative >> n) & 1) << (bits - 1 - n)
    return at


def listed(pack):
    return [pack[7:8, n * 128 : (n + 1) * 128] for n in range(3)]


def choose(relative, near, far):
    at = place(relative >> 1, near.shape[0].bit_length() - 1)
    return jnp.where(relative % 2 == 0, near[at], far[at])


def prepare_kernel(pack, near, far, after, chosen, rows, feat_g, feat_h):
    del after
    m = jnp.max(listed(pack)[1]).astype(jnp.int32)
    chosen[...] = choose(m ^ here("row"), near, far)
    rows[...] = outline(chosen[...], 1.0)
    feat_g[...], feat_h[...] = features(chosen[...])


def pair_kernel(pack, near, far, bpack, rows_b, feat_g, feat_h, after, out_a, out_b, apack, col, *rest):
    del after
    spread_col, sums_a, sums_b, images = rest[0], rest[1:3], rest[3:5], rest[5:7]
    k, _, count = [jnp.max(value).astype(jnp.int32) for value in listed(pack)]

    @pl.when(count > 1)
    def _():
        apack[...] = choose(k ^ here("col"), near, far)
        col[...] = jnp.transpose(outline(apack[...], -2.0))
        interact_both(col, spread_col, rows_b, features(apack[...]), (feat_g, feat_h), images, sums_a, sums_b)
        store_dense(out_a, finish(apack[...], sums_a[0][...], sums_a[1][...]))
        store_dense(out_b, finish(bpack[...], sums_b[0][...], sums_b[1][...]))


def merge_kernel(axis, n_parts, *refs):
    parts, (near, keep, send) = refs[:n_parts], refs[n_parts:]
    at = here(axis)
    total = onward = jnp.zeros(keep.shape, F32)
    for n, part in enumerate(parts):
        relative = 2 * (n_parts - 1 - n)
        k, m, count = listed(near[place(relative >> 1, near.shape[0].bit_length() - 1)])
        if axis == "col":
            target = jnp.where(count > 1, k, -1.0)
        else:
            itself = (k == here("col").astype(F32)) & (m == (at ^ relative).astype(F32))
            target = jnp.where((count > 1) & ~itself, m, -1.0)
        block = part[...]
        total += jnp.where(target == at.astype(F32), block, 0.0)
        onward += jnp.where(target == (at ^ 1).astype(F32), block, 0.0)
    keep[...] = total
    send[...] = onward


def sum_kernel(keep_a, keep_b, part_a, part_b, *refs):
    own, (velocity, stretching) = refs[:-2], refs[-2:]
    total = load_dense(keep_a[...] + keep_b[...] + part_a[...] + part_b[...], 6)
    total += jnp.concatenate([chunk[...] for chunk in own], axis=1)
    velocity[...] = total[0:3]
    stretching[...] = total[3:6]


def own_work(cols):
    return [
        pltpu.VMEM((G_ROWS, cols), F32),
        pltpu.VMEM((H_ROWS, cols), F32),
        *[pltpu.VMEM((UNIT, UNIT), F32)] * 2,
        *[pltpu.VMEM((UNIT, UNIT), BF16)] * 8,
    ]


def pair_work(g):
    return [
        pltpu.VMEM((8, g), F32),
        pltpu.VMEM((g, 8), F32),
        pltpu.VMEM((5, g, 128), F32),
        *[pltpu.VMEM((G_ROWS, g), F32), pltpu.VMEM((H_ROWS, g), F32)] * 2,
        *[pltpu.VMEM((g, 4 * UNIT), BF16)] * 2,
    ]


def swap(block, axis, size, step):
    return lax.ppermute(block, axis, [(i, i ^ step) for i in range(size)])


def spread(block, axis, size):
    return [swap(block, axis, size, s) for s in range(size - 2, 0, -2)] + [block]


def local(n_row, n_col, positions, strengths, radii, pair_list, pair_count):
    g = radii.shape[0]
    part = g // 4
    hbm_spec = pl.BlockSpec(memory_space=pltpu.HBM)
    vmem_spec = pl.BlockSpec(memory_space=pltpu.VMEM)
    params = pltpu.CompilerParams(vmem_limit_bytes=VMEM)
    block = jax.ShapeDtypeStruct((8, g), F32)
    chunk = jax.ShapeDtypeStruct((6, part), F32)
    dense = jax.ShapeDtypeStruct((6 * g // 128, 128), F32)
    chunk_cost = pl.CostEstimate(flops=30 * g * part, bytes_accessed=64 * g, transcendentals=g * part)
    chunk_call = functools.partial(
        pl.pallas_call, scratch_shapes=own_work(part), compiler_params=params, cost_estimate=chunk_cost
    )

    def later(n, after):
        return chunk_call(
            functools.partial(later_kernel, n),
            out_shape=chunk,
            in_specs=[vmem_spec] * 7,
            out_specs=vmem_spec,
            name=f"own_{n}",
        )(pack, *common, after)

    pack = pl.pallas_call(
        pack_kernel,
        out_shape=block,
        in_specs=[hbm_spec] * 5,
        out_specs=vmem_spec,
        scratch_shapes=[
            pltpu.SMEM(pair_list.shape, jnp.int32),
            pltpu.SMEM(pair_count.shape, jnp.int32),
            pltpu.SemaphoreType.DMA((5,)),
        ],
        name="pack_group",
    )(positions, strengths, radii[None], pair_list, pair_count)

    own = []
    near_a, near_b = pack[None], pack[None]
    for stage in range(n_col.bit_length() - 1):
        step_a, step_b = n_col >> (1 + stage), n_row >> (1 + stage)
        far_a = swap(near_a, "col", n_col, step_a)
        if step_b:
            far_b = swap(near_b, "row", n_row, step_b)
        if step_a == 1:
            break
        if stage == 0:
            chunk_0, *common = chunk_call(
                first_kernel,
                out_shape=(
                    chunk,
                    jax.ShapeDtypeStruct((g, Q_ROWS), BF16),
                    jax.ShapeDtypeStruct((g, Q_ROWS), F32),
                    jax.ShapeDtypeStruct((Q_ROWS, g), BF16),
                    jax.ShapeDtypeStruct((G_ROWS, g), BF16),
                    jax.ShapeDtypeStruct((H_ROWS, g), BF16),
                ),
                in_specs=[vmem_spec],
                out_specs=(vmem_spec,) * 6,
                name="own_first",
            )(pack)
            own.append(chunk_0)
        elif stage == 1:
            own.append(later(1, near_a))
            own.append(later(2, near_a))
        arrived = own[-2:] + [far_b]
        runs = [(near_a, far_a)]
        if step_b > 1:
            runs.append((near_b, far_b))
        stacked = pl.pallas_call(
            functools.partial(stack_kernel, len(runs), len(arrived)),
            out_shape=tuple(jax.ShapeDtypeStruct((2 * n.shape[0], 8, g), F32) for n, _ in runs),
            in_specs=[vmem_spec] * (2 * len(runs) + len(arrived)),
            out_specs=(vmem_spec,) * len(runs),
            compiler_params=params,
            name="stack_groups",
        )(*[block for run in runs for block in run], *arrived)
        near_a = stacked[0]
        if len(runs) > 1:
            near_b = stacked[1]

    prepared = pl.pallas_call(
        prepare_kernel,
        out_shape=(
            block,
            block,
            jax.ShapeDtypeStruct((G_ROWS, g), BF16),
            jax.ShapeDtypeStruct((H_ROWS, g), BF16),
        ),
        in_specs=[vmem_spec] * 4,
        out_specs=(vmem_spec,) * 4,
        compiler_params=params,
        cost_estimate=pl.CostEstimate(flops=g * g, bytes_accessed=64 * g, transcendentals=0),
        name="prepare_group",
    )(pack, near_b, far_b, near_a)

    side_a, side_b = pl.pallas_call(
        pair_kernel,
        out_shape=(dense, dense),
        in_specs=[vmem_spec] * 8,
        out_specs=(vmem_spec, vmem_spec),
        scratch_shapes=pair_work(g),
        compiler_params=params,
        cost_estimate=pl.CostEstimate(flops=60 * g * g, bytes_accessed=128 * g, transcendentals=g * g),
        name="listed_pair",
    )(pack, near_a, far_a, *prepared, own[-1])

    def merge(parts, near, axis):
        return pl.pallas_call(
            functools.partial(merge_kernel, axis, len(parts)),
            out_shape=(dense,) * 2,
            in_specs=[vmem_spec] * (len(parts) + 1),
            out_specs=(vmem_spec,) * 2,
            compiler_params=params,
            name="merge_" + axis,
        )(*parts, near)

    parts_a = spread(side_a, "col", n_col)
    parts_b = spread(side_b, "row", n_row)
    keep_b, send_b = merge(parts_b, near_b, "row")
    far_b = swap(send_b, "row", n_row, 1)
    keep_a, send_a = merge(parts_a, near_a, "col")
    far_a = swap(send_a, "col", n_col, 1)
    own.append(later(3, keep_a))

    three = jax.ShapeDtypeStruct((3, g), F32)
    return pl.pallas_call(
        sum_kernel,
        out_shape=(three, three),
        in_specs=[vmem_spec] * 8,
        out_specs=(vmem_spec, vmem_spec),
        compiler_params=params,
        name="sum_parts",
    )(keep_a, keep_b, far_a, far_b, *own)


def solution(mesh):
    placed = (
        P(None, ("row", "col")),
        P(None, ("row", "col")),
        P(("row", "col")),
        P(None, "row", "col", None),
        P("row", "col"),
    )
    return jax.shard_map(
        functools.partial(local, mesh.shape["row"], mesh.shape["col"]),
        mesh=mesh,
        in_specs=placed,
        out_specs=(P(None, ("row", "col")), P(None, ("row", "col"))),
        check_vma=False,
    )
```

```python
import functools
import math

import jax
import jax.numpy as jnp
from jax import lax
from jax.experimental import pallas as pl
from jax.experimental.pallas import tpu as pltpu
from jax.sharding import PartitionSpec as P

F32 = jnp.float32
BF16 = jnp.bfloat16
UNIT = 256
STRIP = 16
G_ROWS = 32
H_ROWS = 96
Q_ROWS = 32
G_SCALE = -1.5 / (4.0 * math.pi)
H_SCALE = 7.5 / (4.0 * math.pi)
VMEM = 48 * 1024 * 1024


def cross(u, v):
    return jnp.concatenate(
        [
            u[1:2] * v[2:3] - u[2:3] * v[1:2],
            u[2:3] * v[0:1] - u[0:1] * v[2:3],
            u[0:1] * v[1:2] - u[1:2] * v[0:1],
        ]
    )


def split(f):
    hi = f.astype(BF16).astype(F32)
    mid = (f - hi).astype(BF16).astype(F32)
    return [hi, mid, (f - hi) - mid]


def features(pack):
    pos = pack[0:3] - 0.5
    st = pack[3:6]
    e0 = jnp.concatenate([st, cross(pos, st), jnp.zeros((2, pack.shape[1]), F32)])
    moments = jnp.concatenate([e0, pos[0:1] * e0, pos[1:2] * e0, pos[2:3] * e0])
    for_g = jnp.concatenate(split(e0) + [jnp.zeros_like(e0)]).astype(BF16)
    return for_g, jnp.concatenate(split(moments)).astype(BF16)


def finish(pack, g, h):
    g = g[0:8] + g[8:16] + g[16:24]
    h = h[0:32] + h[32:64] + h[64:96]
    pos = pack[0:3] - 0.5
    st = pack[3:6]
    dot = jnp.sum(pos * st, axis=0, keepdims=True)
    d = dot * h[0:8] - st[0:1] * h[8:16] - st[1:2] * h[16:24] - st[2:3] * h[24:32]
    vel = G_SCALE * (cross(pos, g[0:3]) - g[3:6])
    stretch = G_SCALE * cross(st, g[0:3]) + H_SCALE * (cross(pos, d[0:3]) - d[3:6])
    return jnp.concatenate([vel, stretch])


def store_dense(out, value):
    rows = value.shape[0]
    for n in range(value.shape[1] // 128):
        out[n * rows : (n + 1) * rows, :] = value[:, n * 128 : (n + 1) * 128]


def load_dense(value, rows):
    return jnp.concatenate([value[n : n + rows] for n in range(0, value.shape[0], rows)], axis=1)


def strip(qq, s, images, r):
    ghi, glo, hhi, hlo = images
    here = slice(r, r + STRIP)
    t = lax.rsqrt(qq)
    t2 = pltpu.reciprocal(qq, approx=True)
    v = s * t2
    t3 = t2 * t
    g = t3 * (v + 2.0 / 3.0)
    h = (t3 * t2) * (v + 0.4)
    high = g.astype(BF16)
    ghi[here] = high
    glo[here] = (g - high.astype(F32)).astype(BF16)
    high = h.astype(BF16)
    hhi[here] = high
    hlo[here] = (h - high.astype(F32)).astype(BF16)


def down(f, image):
    return jnp.dot(f, image, preferred_element_type=F32)


def across(f, image):
    return lax.dot_general(f, image, (((1,), (1,)), ((), ())), preferred_element_type=F32)


def halves(pack):
    return 0.5 * pack[6:7] * pack[6:7]


def distances(pack):
    pos = pack[0:3] - 0.5
    x1, x2, x3 = split(pos)
    norm = jnp.concatenate(split(jnp.sum(pos * pos, axis=0, keepdims=True) + halves(pack)))
    one = jnp.ones_like(norm)
    blank = jnp.zeros((8, pack.shape[1]), F32)
    left = [-2.0 * x for x in (x1, x1, x2, x2, x1, x3)] + [norm, one, blank]
    right = [x1, x2, x1, x2, x3, x1, one, norm, blank]
    return jnp.concatenate(left), jnp.concatenate(right).astype(BF16)


def columns(pack, dist, s_col):
    left, right = distances(pack)
    blank = jnp.zeros((7, pack.shape[1]), F32)
    turned = jnp.transpose(jnp.concatenate([left[:24], halves(pack), blank]))
    s_col[...] = turned
    dist[...] = turned.astype(BF16)
    return right


def interact(dist_a, s_a, dist_b, s_b, feat_a, qq, slots, sums_b):
    for total in sums_b:
        total[...] = jnp.zeros_like(total)

    def products(i, j, images):
        pi, pj = slice(i, i + UNIT), slice(j, j + UNIT)
        steps = []

        def add(total, f, high, low):
            total[:, pj] += down(f, high[...]) + down(f, low[...])

        for kind in range(2):
            f = feat_a[kind][:, pi]
            steps.append(functools.partial(add, sums_b[kind], f, *images[2 * kind : 2 * kind + 2]))
        return steps

    def measure(unit, into):
        i, j = unit
        into[...] = down(dist_a[i : i + UNIT, :], dist_b[:, j : j + UNIT])

    n_strip = UNIT // STRIP
    units = [(i, j) for j in range(0, s_b.shape[1], UNIT) for i in range(0, s_a.shape[0], UNIT)]
    measure(units[0], qq[0])
    waiting = []
    for count, (i, j) in enumerate(units):
        images = slots[count % 2]
        if count + 1 < len(units):
            waiting.insert(0, functools.partial(measure, units[count + 1], qq[(count + 1) % 2]))
        per = n_strip // max(1, len(waiting))
        row = jnp.broadcast_to(s_b[0:1, j : j + UNIT], (STRIP, UNIT))
        for n in range(n_strip):
            at = slice(i + n * STRIP, i + (n + 1) * STRIP)
            here = slice(n * STRIP, (n + 1) * STRIP)
            strip(qq[count % 2][here, :], s_a[at, 24:25] + row, images, n * STRIP)
            if waiting and (n + 1) % per == 0:
                waiting.pop(0)()
        for step in waiting:
            step()
        waiting = products(i, j, images)
    for step in waiting:
        step()


def interact_both(dist_a, s_a, spread_s, dist_b, s_b, feat_a, feat_b, qq, images, sums_a, sums_b):
    rows, n = s_a.shape[0], UNIT
    blocks, chunks = s_b.shape[1] // n, rows // n
    half = rows // 2

    def measure(block, c):
        here, part = slice(c * n, (c + 1) * n), slice(block * n, (block + 1) * n)
        qq[block % 2][here, :] = down(dist_a[here, :], dist_b[:, part])

    def onto_a(block, c, kind):
        here, part = slice(c * n, (c + 1) * n), slice(block * n, (block + 1) * n)
        f = jnp.concatenate([feat_b[kind][:, part]] * 2, axis=1)
        share = across(f, images[block % 2][here, 2 * kind * n : 2 * (kind + 1) * n])
        sums_a[kind][:, here] = share if block == 0 else sums_a[kind][:, here] + share

    def onto_b(block, later, kind):
        here, part = slice(later * half, (later + 1) * half), slice(block * n, (block + 1) * n)
        image = images[block % 2]
        at = 2 * kind * n
        f = jnp.concatenate([feat_a[kind][:, here]] * 2, axis=1)
        share = down(f, jnp.concatenate([image[here, at : at + n], image[here, at + n : at + 2 * n]]))
        sums_b[kind][:, part] = sums_b[kind][:, part] + share if later else share

    for c in range(chunks):
        measure(0, c)
    ready, delayed = [], []
    for block in range(blocks):
        image = images[block % 2]
        part = slice(block * n, (block + 1) * n)
        slots = [image.at[:, m * n : (m + 1) * n] for m in range(4)]
        row = jnp.broadcast_to(s_b[0:1, part], (STRIP, n))
        for c in range(chunks):
            todo, ready, delayed = ready, delayed, []
            if block + 1 < blocks:
                todo.append(functools.partial(measure, block + 1, c))
            n_strip = n // STRIP
            per = max(1, n_strip // max(1, len(todo)))
            for m in range(n_strip):
                here = slice(c * n + m * STRIP, c * n + (m + 1) * STRIP)
                if block == 0:
                    spread_s[here, :] = jnp.broadcast_to(s_a[here, 24:25], (STRIP, 128))
                own = jnp.concatenate([spread_s[here, :]] * (n // 128), axis=1)
                strip(qq[block % 2][here, :], own + row, slots, c * n + m * STRIP)
                if todo and (m + 1) % per == 0:
                    todo.pop(0)()
            for step in todo:
                step()
            for kind in range(2):
                ready.append(functools.partial(onto_a, block, c, kind))
            if (c + 1) % (chunks // 2) == 0:
                later = (c + 1) // (chunks // 2) - 1
                ready.append(functools.partial(onto_b, block, later, 0))
                delayed.append(functools.partial(onto_b, block, later, 1))
    for step in ready + delayed:
        step()


def own_chunk(n, pack, dist, s_col, right, feat, out, sums, qq, slots):
    part = slice(n * out.shape[1], (n + 1) * out.shape[1])
    interact(dist, s_col, right[:, part], halves(pack[:, part]), feat, qq, slots, sums)
    out[...] = finish(pack[:, part], sums[0][...], sums[1][...])


def first_kernel(pack, out, dist, s_col, right, feat_g, feat_h, b_g, b_h, *flat):
    right[...] = columns(pack[...], dist, s_col)
    feat_g[...], feat_h[...] = features(pack[...])
    own_chunk(0, pack, dist, s_col, right, (feat_g, feat_h), out, (b_g, b_h), flat[0:2], (flat[2:6], flat[6:10]))


def later_kernel(n, pack, dist, s_col, right, feat_g, feat_h, after, out, b_g, b_h, *flat):
    del after
    own_chunk(n, pack, dist, s_col, right, (feat_g, feat_h), out, (b_g, b_h), flat[0:2], (flat[2:6], flat[6:10]))


def pack_kernel(positions, strengths, radii, pair_list, pair_count, pack, listed, count, sems):
    copies = [
        pltpu.make_async_copy(pair_list, listed, sems.at[0]),
        pltpu.make_async_copy(pair_count, count, sems.at[1]),
        pltpu.make_async_copy(positions, pack.at[0:3], sems.at[2]),
        pltpu.make_async_copy(strengths, pack.at[3:6], sems.at[3]),
        pltpu.make_async_copy(radii, pack.at[6:7], sems.at[4]),
    ]
    for copy in copies:
        copy.start()
    for copy in copies[:2]:
        copy.wait()
    for n, value in enumerate((listed[0, 0, 0, 1], listed[1, 0, 0, 1], count[0, 0])):
        pack[7:8, n * 128 : (n + 1) * 128] = jnp.full((1, 128), value.astype(F32))
    rest = pack.shape[1] - 3 * 128
    pack[7:8, 3 * 128 :] = jnp.zeros((1, rest), F32)
    for copy in copies[2:]:
        copy.wait()


def here(axis):
    return lax.axis_index(axis).astype(jnp.int32)


def stack_kernel(n_pairs, n_arrived, *refs):
    del n_arrived
    for n in range(n_pairs):
        first, second, both = refs[2 * n], refs[2 * n + 1], refs[n - n_pairs]
        size = first.shape[0]
        both[0:size] = first[...]
        both[size : 2 * size] = second[...]


def place(relative, bits):
    at = 0
    for n in range(bits):
        at += ((relative >> n) & 1) << (bits - 1 - n)
    return at


def listed(pack):
    return [pack[7:8, n * 128 : (n + 1) * 128] for n in range(3)]


def choose(relative, near, far):
    at = place(relative >> 1, near.shape[0].bit_length() - 1)
    return jnp.where(relative % 2 == 0, near[at], far[at])


def prepare_kernel(pack, near, far, after, chosen, right, feat_g, feat_h):
    del after
    m = jnp.max(listed(pack)[1]).astype(jnp.int32)
    chosen[...] = choose(m ^ here("row"), near, far)
    right[...] = distances(chosen[...])[1]
    feat_g[...], feat_h[...] = features(chosen[...])


def pair_kernel(pack, near, far, bpack, right, feat_g, feat_h, after, out_a, out_b, apack, dist, s_col, *rest):
    del after
    spread_s, sums_a, sums_b, qq, images = rest[0], rest[1:3], rest[3:5], rest[5:7], rest[7:9]
    k, _, count = [jnp.max(value).astype(jnp.int32) for value in listed(pack)]

    @pl.when(count > 1)
    def _():
        apack[...] = choose(k ^ here("col"), near, far)
        columns(apack[...], dist, s_col)
        feat_a = features(apack[...])
        interact_both(
            dist, s_col, spread_s, right, halves(bpack[...]), feat_a, (feat_g, feat_h), qq, images, sums_a, sums_b
        )
        store_dense(out_a, finish(apack[...], sums_a[0][...], sums_a[1][...]))
        store_dense(out_b, finish(bpack[...], sums_b[0][...], sums_b[1][...]))


def merge_kernel(axis, n_parts, *refs):
    parts, (near, keep, send) = refs[:n_parts], refs[n_parts:]
    at = here(axis)
    total = onward = jnp.zeros(keep.shape, F32)
    for n, part in enumerate(parts):
        relative = 2 * (n_parts - 1 - n)
        k, m, count = listed(near[place(relative >> 1, near.shape[0].bit_length() - 1)])
        if axis == "col":
            target = jnp.where(count > 1, k, -1.0)
        else:
            itself = (k == here("col").astype(F32)) & (m == (at ^ relative).astype(F32))
            target = jnp.where((count > 1) & ~itself, m, -1.0)
        block = part[...]
        total += jnp.where(target == at.astype(F32), block, 0.0)
        onward += jnp.where(target == (at ^ 1).astype(F32), block, 0.0)
    keep[...] = total
    send[...] = onward


def sum_kernel(keep_a, keep_b, part_a, part_b, *refs):
    own, (velocity, stretching) = refs[:-2], refs[-2:]
    total = load_dense(keep_a[...] + keep_b[...] + part_a[...] + part_b[...], 6)
    total += jnp.concatenate([chunk[...] for chunk in own], axis=1)
    velocity[...] = total[0:3]
    stretching[...] = total[3:6]


def own_work(cols):
    return [
        pltpu.VMEM((G_ROWS, cols), F32),
        pltpu.VMEM((H_ROWS, cols), F32),
        *[pltpu.VMEM((UNIT, UNIT), F32)] * 2,
        *[pltpu.VMEM((UNIT, UNIT), BF16)] * 8,
    ]


def pair_work(g):
    return [
        pltpu.VMEM((8, g), F32),
        pltpu.VMEM((g, Q_ROWS), BF16),
        pltpu.VMEM((g, Q_ROWS), F32),
        pltpu.VMEM((g, 128), F32),
        *[pltpu.VMEM((G_ROWS, g), F32), pltpu.VMEM((H_ROWS, g), F32)] * 2,
        *[pltpu.VMEM((g, UNIT), F32)] * 2,
        *[pltpu.VMEM((g, 4 * UNIT), BF16)] * 2,
    ]


def swap(block, axis, size, step):
    return lax.ppermute(block, axis, [(i, i ^ step) for i in range(size)])


def spread(block, axis, size):
    return [swap(block, axis, size, s) for s in range(size - 2, 0, -2)] + [block]


def local(n_row, n_col, positions, strengths, radii, pair_list, pair_count):
    g = radii.shape[0]
    part = g // 4
    hbm_spec = pl.BlockSpec(memory_space=pltpu.HBM)
    vmem_spec = pl.BlockSpec(memory_space=pltpu.VMEM)
    params = pltpu.CompilerParams(vmem_limit_bytes=VMEM)
    block = jax.ShapeDtypeStruct((8, g), F32)
    chunk = jax.ShapeDtypeStruct((6, part), F32)
    dense = jax.ShapeDtypeStruct((6 * g // 128, 128), F32)
    chunk_cost = pl.CostEstimate(flops=30 * g * part, bytes_accessed=64 * g, transcendentals=g * part)
    chunk_call = functools.partial(
        pl.pallas_call, scratch_shapes=own_work(part), compiler_params=params, cost_estimate=chunk_cost
    )

    def later(n, after):
        return chunk_call(
            functools.partial(later_kernel, n),
            out_shape=chunk,
            in_specs=[vmem_spec] * 7,
            out_specs=vmem_spec,
            name=f"own_{n}",
        )(pack, *common, after)

    pack = pl.pallas_call(
        pack_kernel,
        out_shape=block,
        in_specs=[hbm_spec] * 5,
        out_specs=vmem_spec,
        scratch_shapes=[
            pltpu.SMEM(pair_list.shape, jnp.int32),
            pltpu.SMEM(pair_count.shape, jnp.int32),
            pltpu.SemaphoreType.DMA((5,)),
        ],
        name="pack_group",
    )(positions, strengths, radii[None], pair_list, pair_count)

    own = []
    near_a, near_b = pack[None], pack[None]
    for stage in range(n_col.bit_length() - 1):
        step_a, step_b = n_col >> (1 + stage), n_row >> (1 + stage)
        far_a = swap(near_a, "col", n_col, step_a)
        if step_b:
            far_b = swap(near_b, "row", n_row, step_b)
        if step_a == 1:
            break
        if stage == 0:
            chunk_0, *common = chunk_call(
                first_kernel,
                out_shape=(
                    chunk,
                    jax.ShapeDtypeStruct((g, Q_ROWS), BF16),
                    jax.ShapeDtypeStruct((g, Q_ROWS), F32),
                    jax.ShapeDtypeStruct((Q_ROWS, g), BF16),
                    jax.ShapeDtypeStruct((G_ROWS, g), BF16),
                    jax.ShapeDtypeStruct((H_ROWS, g), BF16),
                ),
                in_specs=[vmem_spec],
                out_specs=(vmem_spec,) * 6,
                name="own_first",
            )(pack)
            own.append(chunk_0)
        elif stage == 1:
            own.append(later(1, near_a))
            own.append(later(2, near_a))
        arrived = own[-2:] + [far_b]
        runs = [(near_a, far_a)]
        if step_b > 1:
            runs.append((near_b, far_b))
        stacked = pl.pallas_call(
            functools.partial(stack_kernel, len(runs), len(arrived)),
            out_shape=tuple(jax.ShapeDtypeStruct((2 * n.shape[0], 8, g), F32) for n, _ in runs),
            in_specs=[vmem_spec] * (2 * len(runs) + len(arrived)),
            out_specs=(vmem_spec,) * len(runs),
            compiler_params=params,
            name="stack_groups",
        )(*[block for run in runs for block in run], *arrived)
        near_a = stacked[0]
        if len(runs) > 1:
            near_b = stacked[1]

    prepared = pl.pallas_call(
        prepare_kernel,
        out_shape=(
            block,
            jax.ShapeDtypeStruct((Q_ROWS, g), BF16),
            jax.ShapeDtypeStruct((G_ROWS, g), BF16),
            jax.ShapeDtypeStruct((H_ROWS, g), BF16),
        ),
        in_specs=[vmem_spec] * 4,
        out_specs=(vmem_spec,) * 4,
        compiler_params=params,
        cost_estimate=pl.CostEstimate(flops=g * g, bytes_accessed=64 * g, transcendentals=0),
        name="prepare_group",
    )(pack, near_b, far_b, near_a)

    side_a, side_b = pl.pallas_call(
        pair_kernel,
        out_shape=(dense, dense),
        in_specs=[vmem_spec] * 8,
        out_specs=(vmem_spec, vmem_spec),
        scratch_shapes=pair_work(g),
        compiler_params=params,
        cost_estimate=pl.CostEstimate(flops=60 * g * g, bytes_accessed=128 * g, transcendentals=g * g),
        name="listed_pair",
    )(pack, near_a, far_a, *prepared, own[-1])

    def merge(parts, near, axis):
        return pl.pallas_call(
            functools.partial(merge_kernel, axis, len(parts)),
            out_shape=(dense,) * 2,
            in_specs=[vmem_spec] * (len(parts) + 1),
            out_specs=(vmem_spec,) * 2,
            compiler_params=params,
            name="merge_" + axis,
        )(*parts, near)

    parts_a = spread(side_a, "col", n_col)
    parts_b = spread(side_b, "row", n_row)
    keep_b, send_b = merge(parts_b, near_b, "row")
    far_b = swap(send_b, "row", n_row, 1)
    keep_a, send_a = merge(parts_a, near_a, "col")
    far_a = swap(send_a, "col", n_col, 1)
    own.append(later(3, keep_a))

    three = jax.ShapeDtypeStruct((3, g), F32)
    return pl.pallas_call(
        sum_kernel,
        out_shape=(three, three),
        in_specs=[vmem_spec] * 8,
        out_specs=(vmem_spec, vmem_spec),
        compiler_params=params,
        name="sum_parts",
    )(keep_a, keep_b, far_a, far_b, *own)


def solution(mesh):
    placed = (
        P(None, ("row", "col")),
        P(None, ("row", "col")),
        P(("row", "col")),
        P(None, "row", "col", None),
        P("row", "col"),
    )
    return jax.shard_map(
        functools.partial(local, mesh.shape["row"], mesh.shape["col"]),
        mesh=mesh,
        in_specs=placed,
        out_specs=(P(None, ("row", "col")), P(None, ("row", "col"))),
        check_vma=False,
    )
```
